128 devices in a mesh: layer: 2 (over x_lo), row: 8 (over y, core), col: 8 (over x_hi, z).
Axes of the slice: x: 4 (x_hi: 2, x_lo: 2; x = x_hi * 2 + x_lo), y: 4, z: 4, core: 2. Of those that a mesh axis runs over, the one named last changes fastest.
Arguments:
- owner_blocks: float32 [256, 64, 2048], P(('layer', 'row', 'col')), may hold values from -0.625 to 0.625
- owner_counts: int32 [8, 16], P('row'), may hold values from 1 to 2, 20 in all within a row
- block_cols: int32 [160, 32], replicated, may hold values from 0 to 159, as said below
- filter_mask: int32 [160, 32], replicated, may hold values 0 or 1
- gamma: float32 [1], replicated, may hold values from 0.5 to 2.5
Outputs:
- purified: float32 [160, 64, 2048], P('row', None, 'col')
The draws below stay inside these ranges and needn't reach their ends.
Inputs may be any that keep to these rules, and one draw needn't show every extreme that they name: `block_cols`: slots g * 4 to (g + 1) * 4 - 1 of each block row hold distinct block columns of g * 20 to (g + 1) * 20 - 1; block row i holds block column i. `owner_counts`: each row sums to 20.
All inputs are finite; a program needn't handle non-finite values.
Results may differ from the reference program's by a relative error of at most 0.0003.
Values sent between devices are 32-bit elements; how exact they have to be, the bound alone decides.
No kernel may reach another device: no remote copies, remote signals or barrier semaphores. Data moves between devices by JAX's collectives and lax.ppermute only.
A program may use at most 256 MiB of HBM per device.

```python
import math
import jax
import jax.numpy as jnp
import numpy as np
from jax import lax

BS = 64
K = 32
BR_DEV = 20
NBR = 160
KP = 4
CAP = 2
OWNER_ROWS = 256
N_LAYER = 2
N_ROW = 8
N_COL = 8


def draw_block_cols(key, part):
    key = jax.random.fold_in(key, 7)
    perm_key, place_key = jax.random.split(key)

    def one_pick(index):
        return jax.random.permutation(jax.random.fold_in(perm_key, index), BR_DEV)[:KP]
    picks = jax.vmap(one_pick)(jnp.arange(NBR * N_COL)).reshape(NBR, N_COL, KP).astype(jnp.int32)
    rows_idx = jnp.arange(NBR, dtype=jnp.int32)
    own_group = rows_idx // BR_DEV
    own_local = rows_idx % BR_DEV
    own_picks = picks[rows_idx, own_group]
    present = jnp.any(own_picks == own_local[:, None], axis=1)
    place = jax.random.randint(place_key, (NBR,), 0, KP)
    group_hit = jnp.arange(N_COL)[None, :] == own_group[:, None]
    slot_hit = jnp.arange(KP)[None, :] == place[:, None]
    replace = group_hit[:, :, None] & slot_hit[:, None, :] & jnp.logical_not(present)[:, None, None]
    picks = jnp.where(replace, own_local[:, None, None], picks)
    columns = picks + (jnp.arange(N_COL, dtype=jnp.int32) * BR_DEV)[None, :, None]
    return columns.reshape(NBR, K).astype(jnp.int32)


def plant(drawn, stream_key, smallest, top_value):
    longest = drawn.shape.index(max(drawn.shape))
    spots = []
    for shift in (0, 1):
        where = [jax.random.randint(jax.random.fold_in(stream_key, axis), (), 0, length) for axis, length in enumerate(drawn.shape)]
        where[longest] = (where[longest] + shift) % drawn.shape[longest]
        spots.append(tuple(where))
    return drawn.at[spots[0]].set(smallest).at[spots[1]].set(top_value)


def level_of(key, shape, cuts, low, largest):
    loudness = 1.0
    for dim, shards_of in cuts:
        heights = jax.random.uniform(jax.random.fold_in(jax.random.fold_in(key, 6), dim), (shards_of,), jnp.float32, low / len(cuts), largest / len(cuts))
        loudness = loudness * jnp.repeat(jnp.exp(heights), shape[dim] // shards_of).reshape((-1,) + (1,) * (len(shape) - 1 - dim))
    return loudness


def split_up(count, total, most, slope):
    weights = [(1 << 20) // math.isqrt(standing ** slope) + 1 for standing in range(2, count + 1)]
    surplus, holding = total - most - (count - 1), [1] * (count - 1)
    while surplus > 0:
        free = [i for i in range(count - 1) if holding[i] < most]
        whole, budget = sum([weights[i] for i in free]), surplus
        for i in free:
            more = min(most - holding[i], max(1, budget * weights[i] // whole), surplus)
            holding[i] = holding[i] + more
            surplus = surplus - more
    return np.array([most] + holding)


def uneven_parts(stream_key, amount, total, limit, slope):
    if amount == 2:
        one = jax.random.randint(stream_key, (), max(1, total - limit), min(limit, total - 1) + 1)
        return jnp.stack([one, total - one])
    sizes = jnp.asarray(split_up(amount, total, limit, slope), jnp.int32)
    pairs = (amount - 1) // 2
    donor, taker = sizes[1:1 + 2 * pairs:2], sizes[2:2 + 2 * pairs:2]
    slack = jnp.minimum(donor - 1, limit - taker)
    moved = jax.random.randint(jax.random.fold_in(stream_key, 1), (pairs,), 0, 1 << 20) % (slack + 1)
    sizes = sizes.at[1:1 + 2 * pairs:2].set(donor - moved).at[2:2 + 2 * pairs:2].set(taker + moved)
    return sizes[jax.random.permutation(jax.random.fold_in(stream_key, 2), amount)]


def noise(rng, shape, deviation, most, cuts=(), kind=jnp.bfloat16):
    result = jax.random.normal(rng, shape, jnp.float32) * deviation
    if len(cuts) > 0:
        result = level_of(rng, shape, cuts, -0.22, 0.18) * result
    return jnp.clip(result, min=-most, max=most).astype(kind)


def setup_inputs(seed: int = 0) -> dict:
    arg_keys = jax.random.split(jax.random.key(seed), 6)
    owner_blocks = noise(arg_keys[0], (OWNER_ROWS, BS, K * BS), (2.0 / (K * BS) ** 0.5), 0.625, ((0, 128),), jnp.float32)
    owner_counts = jax.vmap(lambda own: uneven_parts(own, N_LAYER * N_COL, BR_DEV, CAP, 2))(jax.random.split(arg_keys[1], N_ROW)).reshape((N_ROW, N_LAYER * N_COL)).astype(jnp.int32)
    block_cols = draw_block_cols(jax.random.fold_in(arg_keys[5], 71), 0)
    filter_mask = plant((jax.random.randint(arg_keys[3], (NBR, K), 0, 4) < 3).astype(jnp.int32), jax.random.fold_in(arg_keys[3], 1), 0, 1)
    gamma = jnp.clip(jax.random.uniform(arg_keys[4], (1,), jnp.float32, 0.5, 2.5), 0.5, 2.5)
    return {"owner_blocks": owner_blocks, "owner_counts": owner_counts, "block_cols": block_cols, "filter_mask": filter_mask, "gamma": gamma}


def owner_rows(owner_counts):
    ends = jnp.cumsum(owner_counts, axis=1).astype(jnp.int32)
    starts = ends - owner_counts
    local = jnp.arange(BR_DEV, dtype=jnp.int32)
    which = jnp.sum((ends[:, None, :] <= local[None, :, None]).astype(jnp.int32), axis=2)
    slot = local[None, :] - jnp.take_along_axis(starts, which, axis=1)
    layer_idx = which // N_COL
    col_idx = which % N_COL
    grid_row = jnp.arange(N_ROW, dtype=jnp.int32)[:, None]
    flat = ((layer_idx * N_ROW + grid_row) * N_COL + col_idx) * CAP + slot
    return flat.reshape(-1).astype(jnp.int32)


def filtered_product(left, right, block_cols):
    def one_row(items):
        row_blocks, row_cols = items
        lhs = row_blocks.reshape(BS, K, BS).astype(jnp.float32)
        rhs = jnp.take(right, row_cols, axis=0).reshape(K, BS, K, BS).astype(jnp.float32)
        match = (jnp.take(block_cols, row_cols, axis=0)[:, :, None] == row_cols[None, None, :]).astype(jnp.float32)
        moved = jnp.einsum('kdlc,klm->kdmc', rhs, match, precision=lax.Precision.HIGHEST)
        out = jnp.einsum('akd,kdmc->amc', lhs, moved, precision=lax.Precision.HIGHEST)
        return out.reshape(BS, K * BS)
    return lax.map(one_row, (left, block_cols))


def reference(owner_blocks, owner_counts, block_cols, filter_mask, gamma):
    density = jnp.take(owner_blocks, owner_rows(owner_counts), axis=0)
    keep = filter_mask.astype(jnp.float32)[:, None, :, None]
    square = (filtered_product(density, density, block_cols).reshape(NBR, BS, K, BS) * keep).reshape(NBR, BS, K * BS)
    rows_idx = jnp.arange(NBR, dtype=jnp.int32)
    own = (block_cols == rows_idx[:, None]).astype(jnp.float32)
    unit = (own[:, None, :, None] * jnp.eye(BS, dtype=jnp.float32)[None, :, None, :]).reshape(NBR, BS, K * BS)
    mix = gamma[0]
    mixed = mix * unit + (4.0 - 2.0 * mix) * density + (mix - 3.0) * square
    return filtered_product(square, mixed, block_cols)
```

```python
import functools

import jax
import jax.numpy as jnp
from jax import lax
from jax.experimental import pallas as pl
from jax.experimental.pallas import tpu as pltpu
from jax.sharding import PartitionSpec as P

AXES = ("layer", "row", "col")
N_LAYER, N_Y, N_CORE, N_Q, N_Z = 2, 4, 2, 2, 4
N_GROUP = 8
N_SLOT = 4
HALF = 10


def moves(target):
    pairs = []
    for layer in range(N_LAYER):
        for y in range(N_Y):
            for core in range(N_CORE):
                for q in range(N_Q):
                    for z in range(N_Z):
                        there = target(layer, y, core, q, z)
                        if there is not None:
                            pairs.append((flat(layer, y, core, q, z), flat(*there)))
    return pairs


def flat(layer, y, core, q, z):
    row = (y % N_Y) * N_CORE + core % N_CORE
    return ((layer % N_LAYER) * N_Y * N_CORE + row) * N_Q * N_Z + (q % N_Q) * N_Z + z % N_Z


def source_a(layer, y, core, q, z):
    return core == z % 2


def source_b(layer, y, core, q, z):
    return core == layer ^ q


def always(*place):
    return True


def send(x, who, dlayer=0, dy=0, dcore=0, dq=0, dz=0):
    def target(layer, y, core, q, z):
        if who(layer, y, core, q, z):
            return layer + dlayer, y + dy, core + dcore, q + dq, z + dz
        return None

    return lax.ppermute(x, AXES, moves(target))


def other(who):
    return lambda *place: not who(*place)


def gather_left(own):
    rest = other(source_a)
    far = send(own, source_a, dlayer=1, dq=1)
    below = send(own, source_a, dz=1)
    above = send(own, source_a, dz=-1)
    first = send(below[:HALF], rest, dz=1)
    second = send(above[HALF:], rest, dz=-1)
    far_below = send(far, source_a, dz=1)
    far_above = send(far, source_a, dz=-1)
    far_first = send(first, source_a, dlayer=1, dq=1)
    far_second = send(second, source_a, dlayer=1, dq=1)
    return own, below, first, second, above, far, far_below, far_first, far_second, far_above


def gather_right(own, who):
    below = send(own, who, dy=1)
    above = send(own, who, dy=-1)
    first = send(below[:HALF], who, dy=1)
    second = send(above[HALF:], who, dy=-1)
    return own, above, first, second, below


def gather_right_pair(mine):
    rest = other(source_b)
    own = send(mine, source_b, dlayer=1)
    mine, above, first, second, below = gather_right(mine, source_b)
    own_below = send(own, rest, dy=1)
    own_above = send(own, rest, dy=-1)
    own_first = send(first, source_b, dlayer=1)
    own_second = send(second, source_b, dlayer=1)
    return (mine, above, first, second, below), (own, own_above, own_first, own_second, own_below)


def product_kernel(pair, rows, width, span, pick_ref, flag_ref, *refs):
    left, refs = refs[:10], refs[10:]
    count = 10 if pair else 5
    right, refs = refs[:count], refs[count:]
    out_ref, left_buf, right_buf, high, low, left_sem, right_sem = refs
    own, below, first, second, above, far, far_below, far_first, far_second, far_above = left
    is_source = flag_ref[0] == 1
    is_mine = flag_ref[1] == 1

    def bring(buf, sem, place, part, src, start, begin):
        copy = pltpu.make_async_copy(
            src.at[pl.ds(begin, HALF)], buf.at[place, pl.ds(part * HALF, HALF)], sem.at[place, part]
        )
        if start:
            copy.start()
        else:
            copy.wait()

    def right_start(sources):
        own_, above_, first_, second_, below_ = sources
        for place, src in ((0, own_), (1, above_), (3, below_)):
            for part in range(2):
                bring(right_buf, right_sem, place, part, src, True, part * HALF)
        bring(right_buf, right_sem, 2, 0, first_, True, 0)
        bring(right_buf, right_sem, 2, 1, second_, True, 0)

    if pair:

        @pl.when(is_mine)
        def _():
            right_start(right[:5])

        @pl.when(jnp.logical_not(is_mine))
        def _():
            right_start(right[5:])
    else:
        right_start(right)

    @pl.when(is_source)
    def _():
        for place, src in ((0, own), (2, far)):
            for part in range(2):
                bring(left_buf, left_sem, place, part, src, True, part * HALF)
        for place, part, src in ((1, 0, first), (1, 1, second), (3, 0, far_first), (3, 1, far_second)):
            bring(left_buf, left_sem, place, part, src, True, 0)

    @pl.when(jnp.logical_not(is_source))
    def _():
        for place, src in ((0, below), (1, above), (2, far_below), (3, far_above)):
            for part in range(2):
                bring(left_buf, left_sem, place, part, src, True, part * HALF)

    none = 4 * rows * span
    high[none] = jnp.zeros(high.shape[1:], high.dtype)
    low[none] = jnp.zeros(low.shape[1:], low.dtype)

    for place in range(4):
        for part in range(2):
            bring(right_buf, right_sem, place, part, right[0], False, 0)

            @pl.loop(0, HALF)
            def _(row):
                at = (place * rows + part * HALF + row) * span
                x = right_buf[place, part * HALF + row]
                for v in range(2):
                    piece = x[:, v * 2 * width : (v + 1) * 2 * width]
                    top = piece.astype(jnp.bfloat16).astype(jnp.float32)
                    rest = piece - top
                    high[at + 2 * v] = top.astype(jnp.bfloat16)
                    low[at + 2 * v] = rest.astype(jnp.bfloat16)
                    high[at + 2 * v + 1] = pltpu.roll(top, width, 1).astype(jnp.bfloat16)
                    low[at + 2 * v + 1] = pltpu.roll(rest, width, 1).astype(jnp.bfloat16)

    for place in range(4):
        for part in range(2):
            bring(left_buf, left_sem, place, part, own, False, 0)

    lane = lax.broadcasted_iota(jnp.int32, (width, 2 * width), 1) < width

    @pl.loop(0, rows)
    def _(row):
        both = jnp.zeros((2 * width, span * width), jnp.float32)
        single = jnp.zeros((width, span * width), jnp.float32)
        for place in range(4):
            top_rows, low_rows = [], []
            for k in range(span):
                at = ((row * 4 + place) * span + k) * span
                picks = [pick_ref[at + m] for m in range(span)]
                for table, rows_of in ((high, top_rows), (low, low_rows)):
                    rows_of.append(
                        jnp.concatenate(
                            [
                                jnp.where(lane, table[picks[0]], table[picks[1]]),
                                jnp.where(lane, table[picks[2]], table[picks[3]]),
                            ],
                            axis=1,
                        )
                    )
            x = left_buf[place, row]
            top = x.astype(jnp.bfloat16)
            rest = (x - top.astype(jnp.float32)).astype(jnp.bfloat16)
            both += jnp.dot(
                jnp.concatenate([top, rest], axis=0),
                jnp.concatenate(top_rows, axis=0),
                preferred_element_type=jnp.float32,
            )
            single += jnp.dot(
                top, jnp.concatenate(low_rows, axis=0), preferred_element_type=jnp.float32
            )
        out_ref[row] = both[:width] + both[width:] + single


def product(left, right, picks, flags):
    rows, width, wide = left[0].shape
    span = wide // width
    pair = len(right) == 10
    table = pltpu.VMEM((4 * rows * span + 1, width, 2 * width), jnp.bfloat16)
    return pl.pallas_call(
        functools.partial(product_kernel, pair, rows, width, span),
        out_shape=jax.ShapeDtypeStruct((rows, width, wide), jnp.float32),
        in_specs=[pl.BlockSpec(memory_space=pltpu.SMEM)] * 2
        + [pl.BlockSpec(memory_space=pl.ANY)] * (len(left) + len(right)),
        out_specs=pl.BlockSpec(memory_space=pltpu.VMEM),
        scratch_shapes=[
            pltpu.VMEM((4, rows, width, wide), jnp.float32),
            pltpu.VMEM((4, rows, width, wide), jnp.float32),
            table,
            table,
            pltpu.SemaphoreType.DMA((4, 2)),
            pltpu.SemaphoreType.DMA((4, 2)),
        ],
        compiler_params=pltpu.CompilerParams(vmem_limit_bytes=48 * 1024 * 1024),
        cost_estimate=pl.CostEstimate(flops=10**9, bytes_accessed=12 * 10**6, transcendentals=0),
    )(picks, flags, *left, *right)


def pick_table(block_cols, out_cols, grid_row, grid_col, core, y, q, z, rows, span):
    cols = block_cols.reshape(N_GROUP, rows, N_GROUP, span)
    left_cols = lax.dynamic_slice(block_cols, (grid_row * rows, 0), (rows, N_GROUP * span))
    left_cols = left_cols.reshape(rows, N_GROUP, span)
    source = core == z % 2
    z_first = jnp.where(source, z, (z + N_Z - 1) % N_Z)
    z_second = jnp.where(source, (z + 2) % N_Z, (z + 1) % N_Z)
    groups = jnp.stack(
        [q * N_Z + z_first, q * N_Z + z_second, (1 - q) * N_Z + z_first, (1 - q) * N_Z + z_second]
    )
    names = jnp.arange(N_GROUP, dtype=jnp.int32)
    chosen = (groups[:, None] == names[None, :]).astype(jnp.int32)
    local = left_cols - names[None, :, None] * rows
    slots = jnp.sum(local[:, None] * chosen[None, :, :, None], axis=2)
    right_cols = jnp.sum(
        cols * (names == grid_col).astype(jnp.int32)[None, None, :, None], axis=2
    )
    right_cols = jnp.sum(right_cols[None] * chosen[:, :, None, None], axis=1)
    hit = (slots[..., None] == jnp.arange(rows, dtype=jnp.int32)).astype(jnp.int32)
    found = jnp.sum(hit[..., None] * right_cols[None, :, None], axis=3)
    place = (groups // 2 - y) % N_Y
    base = ((place[None, :, None] * rows + slots) * 2)[..., None]
    match = found[..., :, None] == out_cols[:, None, None, None, :]
    piece = jnp.arange(span, dtype=jnp.int32)
    swap = (piece[:, None] + piece[None, :]) % 2
    entry = (base[..., None] + (piece // 2)[:, None]) * 2 + swap
    none = 4 * rows * span
    picked = none + jnp.sum(jnp.where(match, entry - none, 0), axis=3)
    return picked.reshape(-1).astype(jnp.int32)


def body(owner_blocks, owner_counts, block_cols, filter_mask, gamma):
    layer = lax.axis_index("layer")
    grid_row = lax.axis_index("row")
    grid_col = lax.axis_index("col")
    y, core = grid_row // N_CORE, grid_row % N_CORE
    q, z = grid_col // N_Z, grid_col % N_Z
    part = (layer + q) % 2
    cap, width, _ = owner_blocks.shape
    span = N_SLOT
    rows = block_cols.shape[0] // N_GROUP

    counts = owner_counts[0]
    ends = jnp.cumsum(counts)
    local = jnp.arange(rows, dtype=jnp.int32)
    which = jnp.sum((ends[None, :] <= local[:, None]).astype(jnp.int32), axis=1)
    slot = local - (jnp.take(ends, which) - jnp.take(counts, which))
    source = which * cap + slot
    grouped = owner_blocks.reshape(cap, width, N_GROUP, span * width).transpose(2, 0, 1, 3)
    plain_send = jnp.tile(grouped, (N_LAYER, 1, 1, 1)).reshape(
        N_LAYER * N_GROUP * cap, width, span * width
    )
    plain_got = lax.all_to_all(
        plain_send, ("layer", "col"), split_axis=0, concat_axis=0, tiled=True
    )
    density = jnp.take(plain_got, source, axis=0)

    row_here = 2 * y + part
    out_cols = lax.dynamic_slice(block_cols, (row_here * rows, grid_col * span), (rows, span))
    keep = lax.dynamic_slice(filter_mask, (row_here * rows, grid_col * span), (rows, span))
    picks = pick_table(block_cols, out_cols, row_here, grid_col, core, y, q, z, rows, span)
    flags = jnp.stack([core == z % 2, core == part]).astype(jnp.int32)

    across = send(density, always, dcore=1)
    mine = jnp.where(core == part, density, across)
    right = gather_right(density, always)
    left = gather_left(mine)
    partial_value = product(left, right, picks, flags)
    square = partial_value + send(partial_value, always, dcore=1)
    keep_wide = jnp.repeat(keep.astype(jnp.float32), width, axis=1)[:, None, :]
    square = square * keep_wide
    own = (out_cols == (row_here * rows + local)[:, None]).astype(jnp.float32)
    unit = (own[:, None, :, None] * jnp.eye(width, dtype=jnp.float32)[None, :, None, :]).reshape(
        rows, width, span * width
    )
    mix = gamma[0]
    mixed = mix * unit + (4.0 - 2.0 * mix) * mine + (mix - 3.0) * square

    pair_mine, pair_other = gather_right_pair(mixed)
    left = gather_left(square)
    total = product(left, pair_mine + pair_other, picks, flags)
    total = total + send(total, always, dcore=1)
    swapped = send(total, source_b, dlayer=1)
    return jnp.where(core == part, total, swapped)


def solution(mesh):
    placed = (P(("layer", "row", "col"), None, None), P("row", None), P(), P(), P())
    return jax.shard_map(
        body, mesh=mesh, in_specs=placed, out_specs=P("row", None, "col"), check_vma=False
    )
```

```python
import functools

import jax
import jax.numpy as jnp
from jax import lax
from jax.experimental import pallas as pl
from jax.experimental.pallas import tpu as pltpu
from jax.sharding import PartitionSpec as P

AXES = ("layer", "row", "col")
N_LAYER, N_Y, N_CORE, N_Q, N_Z = 2, 4, 2, 2, 4
N_GROUP = 8
N_SLOT = 4
TABLE_STEP = 4
ROW_STEP = 4
VMEM_BYTES = 60 * 1024 * 1024


def moves(target):
    pairs = []
    for layer in range(N_LAYER):
        for y in range(N_Y):
            for core in range(N_CORE):
                for q in range(N_Q):
                    for z in range(N_Z):
                        there = target(layer, y, core, q, z)
                        if there is not None:
                            pairs.append((flat(layer, y, core, q, z), flat(*there)))
    return pairs


def flat(layer, y, core, q, z):
    row = (y % N_Y) * N_CORE + core % N_CORE
    return ((layer % N_LAYER) * N_Y * N_CORE + row) * N_Q * N_Z + (q % N_Q) * N_Z + z % N_Z


def home_right(layer, y, core, q, z):
    return ((layer ^ q) + y // 2) % 2


def home_left(layer, y, core, q, z):
    return (z + q) % 2


def send(x, target):
    return lax.ppermute(x, AXES, moves(target))


def step(x, dy=0, dz=0):
    return send(x, lambda layer, y, core, q, z: (layer, y + dy, core, q, z + dz))


def swap_cores(x):
    return send(x, lambda layer, y, core, q, z: (layer, y, 1 - core, q, z))


def after(x, *done):
    return lax.optimization_barrier((x, *done))[0]


def first_round(density):
    def right_own(layer, y, core, q, z):
        return layer, y, core + y // 2, q, z

    def left_own(layer, y, core, q, z):
        if core == layer ^ q:
            return layer, y, z + q, q, z
        return layer, y, z + q, 1 - q, z

    def right_across(layer, y, core, q, z):
        return (layer, y + 2, core + y // 2, q, z) if core == layer ^ q else None

    def left_across(layer, y, core, q, z):
        return (layer, y, z + q, q, z + 2) if core == layer ^ q else None

    return (
        send(density, right_across),
        send(density, left_own),
        send(density, left_across),
        send(density, right_own),
    )


def second_round(square, mixed):
    def right_own(layer, y, core, q, z):
        home = home_right(layer, y, core, q, z)
        return (1 - layer, y, core, q, z) if core == home else (layer, y, home, q, z)

    def left_own(layer, y, core, q, z):
        home = home_left(layer, y, core, q, z)
        return (1 - layer, y, core, 1 - q, z) if core == home else (layer, y, home, q, z)

    def right_across(layer, y, core, q, z):
        return (layer, y + 2, core, q, z) if core == home_right(layer, y, core, q, z) else None

    def left_across(layer, y, core, q, z):
        return (layer, y, core, q, z + 2) if core == home_left(layer, y, core, q, z) else None

    return (
        send(mixed, right_across),
        send(square, left_own),
        send(square, left_across),
        send(mixed, right_own),
    )


def gather(right_across, left_own, left_across, right_own):
    def right_pass(layer, y, core, q, z):
        return (1 - layer, y, core, q, z) if core != home_right(layer, y, core, q, z) else None

    def left_pass(layer, y, core, q, z):
        return (1 - layer, y, core, 1 - q, z) if core == home_left(layer, y, core, q, z) else None

    right_now = after(right_own, right_across)
    left_now = after(left_own, right_across, left_across)
    right_below = step(right_now, dy=1)
    right_above = step(right_now, dy=-1)
    left_below = step(left_now, dz=1)
    left_above = step(left_now, dz=-1)
    right_pair = send(right_across, right_pass)
    left_pair = send(after(left_across, right_pair), left_pass)
    left = (left_own, left_below, left_above, left_across, left_pair)
    right = (right_own, right_above, right_across, right_below, right_pair)
    return left, right


def product_kernel(rows, width, span, pick_ref, flag_ref, *refs):
    left, right = refs[:5], refs[5:10]
    out_ref, left_buf, right_buf, high, low, left_sem, right_sem = refs[10:]

    def bring(buf, sem, place, src):
        return pltpu.make_async_copy(src, buf.at[place], sem.at[place])

    for place in (0, 1, 3):
        bring(right_buf, right_sem, place, right[place]).start()

    @pl.when(flag_ref[1] == 1)
    def _():
        bring(right_buf, right_sem, 2, right[2]).start()

    @pl.when(flag_ref[1] == 0)
    def _():
        bring(right_buf, right_sem, 2, right[4]).start()

    for place in (0, 1, 2):
        bring(left_buf, left_sem, place, left[place]).start()

    @pl.when(flag_ref[0] == 1)
    def _():
        bring(left_buf, left_sem, 3, left[3]).start()

    @pl.when(flag_ref[0] == 0)
    def _():
        bring(left_buf, left_sem, 3, left[4]).start()

    none = 4 * rows * span
    high[none] = jnp.zeros(high.shape[1:], high.dtype)
    low[none] = jnp.zeros(low.shape[1:], low.dtype)

    for place in range(4):
        bring(right_buf, right_sem, place, right[place]).wait()

        @pl.loop(0, rows // TABLE_STEP)
        def _(step):
            for j in range(TABLE_STEP):
                row = step * TABLE_STEP + j
                at = (place * rows + row) * span
                x = right_buf[place, row]
                for v in range(2):
                    piece = x[:, v * 2 * width : (v + 1) * 2 * width]
                    top = piece.astype(jnp.bfloat16).astype(jnp.float32)
                    rest = piece - top
                    high[at + 2 * v] = top.astype(jnp.bfloat16)
                    low[at + 2 * v] = rest.astype(jnp.bfloat16)
                    high[at + 2 * v + 1] = pltpu.roll(top, width, 1).astype(jnp.bfloat16)
                    low[at + 2 * v + 1] = pltpu.roll(rest, width, 1).astype(jnp.bfloat16)

    for place in range(4):
        bring(left_buf, left_sem, place, left[0]).wait()

    lane = lax.broadcasted_iota(jnp.int32, (width, 2 * width), 1) < width

    def one_row(row):
        both = jnp.zeros((2 * width, span * width), jnp.float32)
        single = jnp.zeros((width, span * width), jnp.float32)
        for place in range(4):
            top_rows, low_rows = [], []
            for k in range(span):
                at = ((row * 4 + place) * span + k) * span
                picks = [pick_ref[at + m] for m in range(span)]
                for table, rows_of in ((high, top_rows), (low, low_rows)):
                    rows_of.append(
                        jnp.concatenate(
                            [
                                jnp.where(lane, table[picks[0]], table[picks[1]]),
                                jnp.where(lane, table[picks[2]], table[picks[3]]),
                            ],
                            axis=1,
                        )
                    )
            x = left_buf[place, row]
            top = x.astype(jnp.bfloat16)
            rest = (x - top.astype(jnp.float32)).astype(jnp.bfloat16)
            both += jnp.dot(
                jnp.concatenate([top, rest], axis=0),
                jnp.concatenate(top_rows, axis=0),
                preferred_element_type=jnp.float32,
            )
            single += jnp.dot(
                top, jnp.concatenate(low_rows, axis=0), preferred_element_type=jnp.float32
            )
        out_ref[row] = both[:width] + both[width:] + single

    @pl.loop(0, rows // ROW_STEP)
    def _(step):
        for j in range(ROW_STEP):
            one_row(step * ROW_STEP + j)


def product(left, right, picks, flags):
    rows, width, wide = left[0].shape
    span = wide // width
    table = pltpu.VMEM((4 * rows * span + 1, width, 2 * width), jnp.bfloat16)
    return pl.pallas_call(
        functools.partial(product_kernel, rows, width, span),
        out_shape=jax.ShapeDtypeStruct((rows, width, wide), jnp.float32),
        in_specs=[pl.BlockSpec(memory_space=pltpu.SMEM)] * 2
        + [pl.BlockSpec(memory_space=pl.ANY)] * (len(left) + len(right)),
        out_specs=pl.BlockSpec(memory_space=pltpu.VMEM),
        scratch_shapes=[
            pltpu.VMEM((4, rows, width, wide), jnp.float32),
            pltpu.VMEM((4, rows, width, wide), jnp.float32),
            table,
            table,
            pltpu.SemaphoreType.DMA((4,)),
            pltpu.SemaphoreType.DMA((4,)),
        ],
        compiler_params=pltpu.CompilerParams(vmem_limit_bytes=VMEM_BYTES),
        cost_estimate=pl.CostEstimate(flops=10**9, bytes_accessed=12 * 10**6, transcendentals=0),
    )(picks, flags, *left, *right)


def pick_table(block_cols, out_cols, grid_row, grid_col, core, y, z, rows, span):
    cols = block_cols.reshape(N_GROUP, rows, N_GROUP, span)
    left_cols = lax.dynamic_slice(block_cols, (grid_row * rows, 0), (rows, N_GROUP * span))
    left_cols = left_cols.reshape(rows, N_GROUP, span)
    z_from = (z + jnp.array([0, 3, 1, 2], dtype=jnp.int32)) % N_Z
    groups = (core + z_from) % 2 * N_Z + z_from
    names = jnp.arange(N_GROUP, dtype=jnp.int32)
    chosen = (groups[:, None] == names[None, :]).astype(jnp.int32)
    local = left_cols - names[None, :, None] * rows
    slots = jnp.sum(local[:, None] * chosen[None, :, :, None], axis=2)
    right_cols = jnp.sum(
        cols * (names == grid_col).astype(jnp.int32)[None, None, :, None], axis=2
    )
    right_cols = jnp.sum(right_cols[None] * chosen[:, :, None, None], axis=1)
    hit = (slots[..., None] == jnp.arange(rows, dtype=jnp.int32)).astype(jnp.int32)
    found = jnp.sum(hit[..., None] * right_cols[None, :, None], axis=3)
    place = (groups // 2 - y) % N_Y
    base = ((place[None, :, None] * rows + slots) * 2)[..., None]
    match = found[..., :, None] == out_cols[:, None, None, None, :]
    piece = jnp.arange(span, dtype=jnp.int32)
    swap = (piece[:, None] + piece[None, :]) % 2
    entry = (base[..., None] + (piece // 2)[:, None]) * 2 + swap
    none = 4 * rows * span
    picked = none + jnp.sum(jnp.where(match, entry - none, 0), axis=3)
    return picked.reshape(-1).astype(jnp.int32)


def body(owner_blocks, owner_counts, block_cols, filter_mask, gamma):
    layer = lax.axis_index("layer")
    grid_row = lax.axis_index("row")
    grid_col = lax.axis_index("col")
    y, core = grid_row // N_CORE, grid_row % N_CORE
    q, z = grid_col // N_Z, grid_col % N_Z
    part = (layer + q) % 2
    cap, width, _ = owner_blocks.shape
    span = N_SLOT
    rows = block_cols.shape[0] // N_GROUP

    counts = owner_counts[0]
    ends = jnp.cumsum(counts)
    local = jnp.arange(rows, dtype=jnp.int32)
    which = jnp.sum((ends[None, :] <= local[:, None]).astype(jnp.int32), axis=1)
    slot = local - (jnp.take(ends, which) - jnp.take(counts, which))
    source = which * cap + slot
    grouped = owner_blocks.reshape(cap, width, N_GROUP, span * width).transpose(2, 0, 1, 3)
    plain_send = jnp.tile(grouped, (N_LAYER, 1, 1, 1)).reshape(
        N_LAYER * N_GROUP * cap, width, span * width
    )
    plain_got = lax.all_to_all(
        plain_send, ("layer", "col"), split_axis=0, concat_axis=0, tiled=True
    )
    row_here = 2 * y + part
    out_cols = lax.dynamic_slice(block_cols, (row_here * rows, grid_col * span), (rows, span))
    keep = lax.dynamic_slice(filter_mask, (row_here * rows, grid_col * span), (rows, span))
    picks = pick_table(block_cols, out_cols, row_here, grid_col, core, y, z, rows, span)
    flags = jnp.stack([core == (z + q) % 2, core != (part + y // 2) % 2]).astype(jnp.int32)

    plain_got, picks, flags = lax.optimization_barrier((plain_got, picks, flags))
    density = jnp.take(plain_got, source, axis=0)

    left, right = gather(*first_round(density))
    mine = jnp.where(core == part, density, swap_cores(after(density, left[4])))
    partial_value = product(left, right, picks, flags)
    square = partial_value + swap_cores(partial_value)
    keep_wide = jnp.repeat(keep.astype(jnp.float32), width, axis=1)[:, None, :]
    square = square * keep_wide
    own = (out_cols == (row_here * rows + local)[:, None]).astype(jnp.float32)
    unit = (own[:, None, :, None] * jnp.eye(width, dtype=jnp.float32)[None, :, None, :]).reshape(
        rows, width, span * width
    )
    mix = gamma[0]
    mixed = mix * unit + (4.0 - 2.0 * mix) * mine + (mix - 3.0) * square

    left, right = gather(*second_round(square, mixed))
    total = product(left, right, picks, flags)
    total = total + swap_cores(total)

    def output(layer, y, core, q, z):
        return (1 - layer, y, core, q, z) if core == layer ^ q else None

    swapped = send(total, output)
    return jnp.where(core == part, total, swapped)


def solution(mesh):
    placed = (P(("layer", "row", "col"), None, None), P("row", None), P(), P(), P())
    return jax.shard_map(
        body, mesh=mesh, in_specs=placed, out_specs=P("row", None, "col"), check_vma=False
    )
```

```python
import functools

import jax
import jax.numpy as jnp
from jax import lax
from jax.experimental import pallas as pl
from jax.experimental.pallas import tpu as pltpu
from jax.sharding import PartitionSpec as P

AXES = ("layer", "row", "col")
N_LAYER, N_Y, N_CORE, N_Q, N_Z = 2, 4, 2, 2, 4
N_GROUP = 8
N_SLOT = 4
TABLE_STEP = 10
ROW_STEP = 5
TABLE_BYTES = 20 * 1024 * 1024
PRODUCT_BYTES = 20 * 1024 * 1024


def moves(target):
    pairs = []
    for layer in range(N_LAYER):
        for y in range(N_Y):
            for core in range(N_CORE):
                for q in range(N_Q):
                    for z in range(N_Z):
                        there = target(layer, y, core, q, z)
                        if there is not None:
                            pairs.append((flat(layer, y, core, q, z), flat(*there)))
    return pairs


def flat(layer, y, core, q, z):
    row = (y % N_Y) * N_CORE + core % N_CORE
    return ((layer % N_LAYER) * N_Y * N_CORE + row) * N_Q * N_Z + (q % N_Q) * N_Z + z % N_Z


def home_right(layer, y, core, q, z):
    return ((layer ^ q) + y // 2) % 2


def home_left(layer, y, core, q, z):
    return (z + q) % 2


def send(x, target):
    return lax.ppermute(x, AXES, moves(target))


def step(x, dy=0, dz=0):
    return send(x, lambda layer, y, core, q, z: (layer, y + dy, core, q, z + dz))


def swap_cores(x):
    return send(x, lambda layer, y, core, q, z: (layer, y, 1 - core, q, z))


def after(x, *done):
    return lax.optimization_barrier((x, *done))[0]


def left_pass(layer, y, core, q, z):
    return (1 - layer, y, core, 1 - q, z) if core == home_left(layer, y, core, q, z) else None


def gather_first(density):
    def right_step(dy):
        return lambda layer, y, core, q, z: (layer, y + dy, core + y // 2, q, z)

    def left_own(layer, y, core, q, z):
        if core == layer ^ q:
            return layer, y, z + q, q, z
        return layer, y, z + q, 1 - q, z

    def left_across(layer, y, core, q, z):
        return (layer, y, z + q, q, z + 2) if core == layer ^ q else None

    half = density.shape[0] // 2
    below = send(density, right_step(1))
    above = send(density, right_step(-1))
    left = send(density, left_own)
    across = send(density, left_across)
    swapped = swap_cores(density)
    left_now = after(left, across, swapped)
    left_below = step(left_now, dz=1)
    left_above = step(left_now, dz=-1)
    left_pair = send(across, left_pass)
    first = step(below[:half], dy=1)
    second = step(above[half:], dy=-1)
    return (left, left_below, left_above, across, left_pair), (density, above, first, below, second, swapped)


def gather_second(square, mixed):
    def right_own(layer, y, core, q, z):
        home = home_right(layer, y, core, q, z)
        return (1 - layer, y, core, q, z) if core == home else (layer, y, home, q, z)

    def left_own(layer, y, core, q, z):
        home = home_left(layer, y, core, q, z)
        return (1 - layer, y, core, 1 - q, z) if core == home else (layer, y, home, q, z)

    def right_across(layer, y, core, q, z):
        return (layer, y + 2, core, q, z) if core == home_right(layer, y, core, q, z) else None

    def left_across(layer, y, core, q, z):
        return (layer, y, core, q, z + 2) if core == home_left(layer, y, core, q, z) else None

    def right_pass(layer, y, core, q, z):
        return (1 - layer, y, core, q, z) if core != home_right(layer, y, core, q, z) else None

    own = send(mixed, right_own)
    left = send(square, left_own)
    across = send(mixed, right_across)
    left_across = send(square, left_across)
    left_now = after(left, own)
    below = step(own, dy=1)
    above = step(own, dy=-1)
    left_below = step(left_now, dz=1)
    left_above = step(left_now, dz=-1)
    pair = send(after(across, left_across, own, left), right_pass)
    left_pair = send(after(left_across, pair), left_pass)
    return (left, left_below, left_above, left_across, left_pair), (own, above, across, below, pair)


def table_kernel(rows, width, span, flag_ref, *refs):
    right = refs[:-4]
    high, low, right_buf, right_sem = refs[-4:]

    def bring(place, src):
        return pltpu.make_async_copy(src, right_buf.at[place], right_sem.at[place])

    for place in (1, 3):
        bring(place, right[place]).start()

    half = right[2].shape[0]
    if half < rows:
        first = pltpu.make_async_copy(right[2], right_buf.at[2, pl.ds(0, half)], right_sem.at[2])
        second = pltpu.make_async_copy(right[4], right_buf.at[2, pl.ds(half, half)], right_sem.at[4])
        first.start()
        second.start()

        @pl.when(flag_ref[2] == 0)
        def _():
            bring(0, right[0]).start()

        @pl.when(flag_ref[2] == 1)
        def _():
            bring(0, right[5]).start()
    else:
        bring(0, right[0]).start()

        @pl.when(flag_ref[1] == 1)
        def _():
            bring(2, right[2]).start()

        @pl.when(flag_ref[1] == 0)
        def _():
            bring(2, right[4]).start()

    none = 4 * rows * span
    high[none] = jnp.zeros(high.shape[1:], high.dtype)
    low[none] = jnp.zeros(low.shape[1:], low.dtype)

    for place in (1, 3, 0, 2):
        if place == 2 and half < rows:
            first.wait()
            second.wait()
        else:
            bring(place, right[place]).wait()

        @pl.loop(0, rows // TABLE_STEP)
        def _(step):
            for j in range(TABLE_STEP):
                row = step * TABLE_STEP + j
                at = (place * rows + row) * span
                x = right_buf[place, row]
                for v in range(2):
                    piece = x[:, v * 2 * width : (v + 1) * 2 * width]
                    for swap, part in enumerate((piece, pltpu.roll(piece, width, 1))):
                        top = part.astype(jnp.bfloat16)
                        high[at + 2 * v + swap] = top
                        low[at + 2 * v + swap] = (part - top.astype(jnp.float32)).astype(jnp.bfloat16)


def table(right, flags):
    rows, width, wide = right[0].shape
    span = wide // width
    kind = pltpu.VMEM((4 * rows * span + 1, width, 2 * width), jnp.bfloat16)
    return pl.pallas_call(
        functools.partial(table_kernel, rows, width, span),
        out_shape=(kind, kind),
        in_specs=[pl.BlockSpec(memory_space=pltpu.SMEM)]
        + [pl.BlockSpec(memory_space=pl.ANY)] * len(right),
        out_specs=(pl.BlockSpec(memory_space=pltpu.VMEM),) * 2,
        scratch_shapes=[
            pltpu.VMEM((4, rows, width, wide), jnp.float32),
            pltpu.SemaphoreType.DMA((5,)),
        ],
        compiler_params=pltpu.CompilerParams(vmem_limit_bytes=TABLE_BYTES),
        cost_estimate=pl.CostEstimate(flops=4 * 10**9, bytes_accessed=10**7, transcendentals=0),
    )(flags, *right)


def product_kernel(rows, width, span, pick_ref, flag_ref, high, low, *refs):
    left = refs[:5]
    out_ref, left_buf, left_sem = refs[5:]

    def bring(place, src):
        return pltpu.make_async_copy(src, left_buf.at[place], left_sem.at[place])

    for place in (0, 1, 2):
        bring(place, left[place]).start()

    @pl.when(flag_ref[0] == 1)
    def _():
        bring(3, left[3]).start()

    @pl.when(flag_ref[0] == 0)
    def _():
        bring(3, left[4]).start()

    for place in range(4):
        bring(place, left[0]).wait()

    lane = lax.broadcasted_iota(jnp.int32, (width, 2 * width), 1) < width

    def one_row(row):
        both = jnp.zeros((2 * width, span * width), jnp.float32)
        single = jnp.zeros((width, span * width), jnp.float32)
        for place in range(4):
            top_rows, low_rows = [], []
            for k in range(span):
                at = ((row * 4 + place) * span + k) * span
                picks = [pick_ref[at + m] for m in range(span)]
                for entries, rows_of in ((high, top_rows), (low, low_rows)):
                    rows_of.append(
                        jnp.concatenate(
                            [
                                jnp.where(lane, entries[picks[0]], entries[picks[1]]),
                                jnp.where(lane, entries[picks[2]], entries[picks[3]]),
                            ],
                            axis=1,
                        )
                    )
            x = left_buf[place, row]
            top = x.astype(jnp.bfloat16)
            rest = (x - top.astype(jnp.float32)).astype(jnp.bfloat16)
            both += jnp.dot(
                jnp.concatenate([top, rest], axis=0),
                jnp.concatenate(top_rows, axis=0),
                preferred_element_type=jnp.float32,
            )
            single += jnp.dot(
                top, jnp.concatenate(low_rows, axis=0), preferred_element_type=jnp.float32
            )
        out_ref[row] = both[:width] + both[width:] + single

    @pl.loop(0, rows // ROW_STEP)
    def _(step):
        for j in range(ROW_STEP):
            one_row(step * ROW_STEP + j)


def product(left, right, picks, flags):
    rows, width, wide = left[0].shape
    span = wide // width
    high, low = (pltpu.with_memory_space_constraint(x, pltpu.VMEM) for x in table(right, flags))
    return pl.pallas_call(
        functools.partial(product_kernel, rows, width, span),
        out_shape=jax.ShapeDtypeStruct((rows, width, wide), jnp.float32),
        in_specs=[pl.BlockSpec(memory_space=pltpu.SMEM)] * 2
        + [pl.BlockSpec(memory_space=pltpu.VMEM)] * 2
        + [pl.BlockSpec(memory_space=pl.ANY)] * len(left),
        out_specs=pl.BlockSpec(memory_space=pltpu.VMEM),
        scratch_shapes=[
            pltpu.VMEM((4, rows, width, wide), jnp.float32),
            pltpu.SemaphoreType.DMA((4,)),
        ],
        compiler_params=pltpu.CompilerParams(vmem_limit_bytes=PRODUCT_BYTES),
        cost_estimate=pl.CostEstimate(flops=8 * 10**9, bytes_accessed=10**7, transcendentals=0),
    )(picks, flags, high, low, *left)


def pick_table(block_cols, out_cols, grid_row, grid_col, core, y, z, rows, span):
    cols = block_cols.reshape(N_GROUP, rows, N_GROUP, span)
    left_cols = lax.dynamic_slice(block_cols, (grid_row * rows, 0), (rows, N_GROUP * span))
    left_cols = left_cols.reshape(rows, N_GROUP, span)
    z_from = (z + jnp.array([0, 3, 1, 2], dtype=jnp.int32)) % N_Z
    groups = (core + z_from) % 2 * N_Z + z_from
    names = jnp.arange(N_GROUP, dtype=jnp.int32)
    chosen = (groups[:, None] == names[None, :]).astype(jnp.int32)
    local = left_cols - names[None, :, None] * rows
    slots = jnp.sum(local[:, None] * chosen[None, :, :, None], axis=2)
    right_cols = jnp.sum(
        cols * (names == grid_col).astype(jnp.int32)[None, None, :, None], axis=2
    )
    right_cols = jnp.sum(right_cols[None] * chosen[:, :, None, None], axis=1)
    hit = (slots[..., None] == jnp.arange(rows, dtype=jnp.int32)).astype(jnp.int32)
    found = jnp.sum(hit[..., None] * right_cols[None, :, None], axis=3)
    place = (groups // 2 - y) % N_Y
    base = ((place[None, :, None] * rows + slots) * 2)[..., None]
    match = found[..., :, None] == out_cols[:, None, None, None, :]
    piece = jnp.arange(span, dtype=jnp.int32)
    swap = (piece[:, None] + piece[None, :]) % 2
    entry = (base[..., None] + (piece // 2)[:, None]) * 2 + swap
    none = 4 * rows * span
    picked = none + jnp.sum(jnp.where(match, entry - none, 0), axis=3)
    return picked.reshape(-1).astype(jnp.int32)


def body(owner_blocks, owner_counts, block_cols, filter_mask, gamma):
    layer = lax.axis_index("layer")
    grid_row = lax.axis_index("row")
    grid_col = lax.axis_index("col")
    y, core = grid_row // N_CORE, grid_row % N_CORE
    q, z = grid_col // N_Z, grid_col % N_Z
    part = (layer + q) % 2
    cap, width, _ = owner_blocks.shape
    span = N_SLOT
    rows = block_cols.shape[0] // N_GROUP

    counts = owner_counts[0]
    ends = jnp.cumsum(counts)
    local = jnp.arange(rows, dtype=jnp.int32)
    which = jnp.sum((ends[None, :] <= local[:, None]).astype(jnp.int32), axis=1)
    slot = local - (jnp.take(ends, which) - jnp.take(counts, which))
    source = which * cap + slot
    grouped = owner_blocks.reshape(cap, width, N_GROUP, span * width).transpose(2, 0, 1, 3)
    plain_send = jnp.tile(grouped, (N_LAYER, 1, 1, 1)).reshape(
        N_LAYER * N_GROUP * cap, width, span * width
    )
    plain_got = lax.all_to_all(
        plain_send, ("layer", "col"), split_axis=0, concat_axis=0, tiled=True
    )
    row_here = 2 * y + part
    out_cols = lax.dynamic_slice(block_cols, (row_here * rows, grid_col * span), (rows, span))
    keep = lax.dynamic_slice(filter_mask, (row_here * rows, grid_col * span), (rows, span))
    picks = pick_table(block_cols, out_cols, row_here, grid_col, core, y, z, rows, span)
    flags = jnp.stack([core == (z + q) % 2, core != (part + y // 2) % 2, y >= 2]).astype(jnp.int32)

    keep_wide = jnp.repeat(keep.astype(jnp.float32), width, axis=1)[:, None, :]
    own = (out_cols == (row_here * rows + local)[:, None]).astype(jnp.float32)
    plain_got, source, picks, flags, keep_wide, own = lax.optimization_barrier(
        (plain_got, source, picks, flags, keep_wide, own)
    )
    density = plain_got.at[source].get(mode="promise_in_bounds")

    left, right = gather_first(density)
    mine = jnp.where(core == part, density, right[5])
    partial_value = product(left, right, picks, flags)
    square = partial_value + swap_cores(partial_value)
    square = square * keep_wide
    unit = (own[:, None, :, None] * jnp.eye(width, dtype=jnp.float32)[None, :, None, :]).reshape(
        rows, width, span * width
    )
    mix = gamma[0]
    mixed = mix * unit + (4.0 - 2.0 * mix) * mine + (mix - 3.0) * square

    left, right = gather_second(square, mixed)

    def output(layer, y, core, q, z):
        return (1 - layer, y, core, q, z) if core == layer ^ q else None

    total = product(left, right, picks, flags)
    total = total + swap_cores(total)
    return jnp.where(core == part, total, send(total, output))


def solution(mesh):
    placed = (P(("layer", "row", "col"), None, None), P("row", None), P(), P(), P())
    return jax.shard_map(
        body, mesh=mesh, in_specs=placed, out_specs=P("row", None, "col"), check_vma=False
    )
```

```python
import functools

import jax
import jax.numpy as jnp
from jax import lax
from jax.experimental import pallas as pl
from jax.experimental.pallas import tpu as pltpu
from jax.sharding import PartitionSpec as P

AXES = ("layer", "row", "col")
N_LAYER, N_Y, N_CORE, N_Q, N_Z = 2, 4, 2, 2, 4
N_GROUP = 8
N_SLOT = 4
TABLE_STEP = 10
ROW_STEP = 5
TABLE_BYTES = 8 * 1024 * 1024
PRODUCT_BYTES = 10 * 1024 * 1024


def moves(target):
    pairs = []
    for layer in range(N_LAYER):
        for y in range(N_Y):
            for core in range(N_CORE):
                for q in range(N_Q):
                    for z in range(N_Z):
                        there = target(layer, y, core, q, z)
                        if there is not None:
                            pairs.append((flat(layer, y, core, q, z), flat(*there)))
    return pairs


def flat(layer, y, core, q, z):
    row = (y % N_Y) * N_CORE + core % N_CORE
    return ((layer % N_LAYER) * N_Y * N_CORE + row) * N_Q * N_Z + (q % N_Q) * N_Z + z % N_Z


def home_right(layer, y, core, q, z):
    return ((layer ^ q) + y // 2) % 2


def home_left(layer, y, core, q, z):
    return (z + q) % 2


def send(x, target):
    return lax.ppermute(x, AXES, moves(target))


def step(x, dy=0, dz=0):
    return send(x, lambda layer, y, core, q, z: (layer, y + dy, core, q, z + dz))


def swap_cores(x):
    return send(x, lambda layer, y, core, q, z: (layer, y, 1 - core, q, z))


def after(x, *done):
    return lax.optimization_barrier((x, *done))[0]


def left_pass(layer, y, core, q, z):
    return (1 - layer, y, core, 1 - q, z) if core == home_left(layer, y, core, q, z) else None


def gather_first(density):
    def right_step(dy):
        return lambda layer, y, core, q, z: (layer, y + dy, core + y // 2, q, z)

    def left_own(layer, y, core, q, z):
        if core == layer ^ q:
            return layer, y, z + q, q, z
        return layer, y, z + q, 1 - q, z

    def left_across(layer, y, core, q, z):
        return (layer, y, z + q, q, z + 2) if core == layer ^ q else None

    half = density.shape[0] // 2
    below = send(density, right_step(1))
    above = send(density, right_step(-1))
    left = send(density, left_own)
    across = send(density, left_across)
    swapped = swap_cores(density)
    left_now = after(left, across, swapped)
    left_below = step(left_now, dz=1)
    left_above = step(left_now, dz=-1)
    left_pair = send(across, left_pass)
    first = step(below[:half], dy=1)
    second = step(above[half:], dy=-1)
    return (left, left_below, left_above, across, left_pair), (density, above, first, below, second, swapped)


def gather_second(square, mixed):
    def right_own(layer, y, core, q, z):
        home = home_right(layer, y, core, q, z)
        return (1 - layer, y, core, q, z) if core == home else (layer, y, home, q, z)

    def left_own(layer, y, core, q, z):
        home = home_left(layer, y, core, q, z)
        return (1 - layer, y, core, 1 - q, z) if core == home else (layer, y, home, q, z)

    def right_across(layer, y, core, q, z):
        return (layer, y + 2, core, q, z) if core == home_right(layer, y, core, q, z) else None

    def left_across(layer, y, core, q, z):
        return (layer, y, core, q, z + 2) if core == home_left(layer, y, core, q, z) else None

    def right_pass(layer, y, core, q, z):
        return (1 - layer, y, core, q, z) if core != home_right(layer, y, core, q, z) else None

    own = send(mixed, right_own)
    left = send(square, left_own)
    across = send(mixed, right_across)
    left_across = send(square, left_across)
    left_now = after(left, own)
    below = step(own, dy=1)
    above = step(own, dy=-1)
    left_below = step(left_now, dz=1)
    left_above = step(left_now, dz=-1)
    pair = send(after(across, own), right_pass)
    left_pair = send(after(left_across, pair), left_pass)
    return (left, left_below, left_above, left_across, left_pair), (own, above, across, below, pair)


def table_kernel(rows, width, span, flag_ref, *refs):
    right = refs[:-4]
    high, low, right_buf, right_sem = refs[-4:]

    def bring(place, src):
        return pltpu.make_async_copy(src, right_buf.at[place], right_sem.at[place])

    for place in (1, 3):
        bring(place, right[place]).start()

    half = right[2].shape[0]
    if half < rows:
        first = pltpu.make_async_copy(right[2], right_buf.at[2, pl.ds(0, half)], right_sem.at[2])
        second = pltpu.make_async_copy(right[4], right_buf.at[2, pl.ds(half, half)], right_sem.at[4])
        first.start()
        second.start()

        @pl.when(flag_ref[2] == 0)
        def _():
            bring(0, right[0]).start()

        @pl.when(flag_ref[2] == 1)
        def _():
            bring(0, right[5]).start()
    else:
        bring(0, right[0]).start()

        @pl.when(flag_ref[1] == 1)
        def _():
            bring(2, right[2]).start()

        @pl.when(flag_ref[1] == 0)
        def _():
            bring(2, right[4]).start()

    none = 4 * rows * span
    high[none] = jnp.zeros(high.shape[1:], high.dtype)
    low[none] = jnp.zeros(low.shape[1:], low.dtype)

    for place in (1, 3, 0, 2):
        if place == 2 and half < rows:
            first.wait()
            second.wait()
        else:
            bring(place, right[place]).wait()

        @pl.loop(0, rows // TABLE_STEP)
        def _(step):
            for j in range(TABLE_STEP):
                row = step * TABLE_STEP + j
                at = (place * rows + row) * span
                x = right_buf[place, row]
                for v in range(2):
                    piece = x[:, v * 2 * width : (v + 1) * 2 * width]
                    for swap, part in enumerate((piece, pltpu.roll(piece, width, 1))):
                        top = part.astype(jnp.bfloat16)
                        high[at + 2 * v + swap] = top
                        low[at + 2 * v + swap] = (part - top.astype(jnp.float32)).astype(jnp.bfloat16)


def table(right, flags):
    rows, width, wide = right[0].shape
    span = wide // width
    kind = pltpu.VMEM((4 * rows * span + 1, width, 2 * width), jnp.bfloat16)
    return pl.pallas_call(
        functools.partial(table_kernel, rows, width, span),
        out_shape=(kind, kind),
        in_specs=[pl.BlockSpec(memory_space=pltpu.SMEM)]
        + [pl.BlockSpec(memory_space=pl.ANY)] * len(right),
        out_specs=(pl.BlockSpec(memory_space=pltpu.VMEM),) * 2,
        scratch_shapes=[
            pltpu.VMEM((4, rows, width, wide), jnp.float32),
            pltpu.SemaphoreType.DMA((5,)),
        ],
        compiler_params=pltpu.CompilerParams(vmem_limit_bytes=TABLE_BYTES),
        cost_estimate=pl.CostEstimate(flops=4 * 10**9, bytes_accessed=10**7, transcendentals=0),
    )(flags, *right)


def product_kernel(begin, end, width, span, pick_ref, flag_ref, high, low, *refs):
    left = refs[:5]
    out_ref, left_buf, left_sem = refs[5:]

    def bring(place, src):
        rows_here = src.at[pl.ds(begin, end - begin)]
        return pltpu.make_async_copy(rows_here, left_buf.at[place], left_sem.at[place])

    for place in (0, 1, 2):
        bring(place, left[place]).start()

    @pl.when(flag_ref[0] == 1)
    def _():
        bring(3, left[3]).start()

    @pl.when(flag_ref[0] == 0)
    def _():
        bring(3, left[4]).start()

    for place in range(4):
        bring(place, left[0]).wait()

    lane = lax.broadcasted_iota(jnp.int32, (width, 2 * width), 1) < width

    def one_row(row):
        both = jnp.zeros((2 * width, span * width), jnp.float32)
        single = jnp.zeros((width, span * width), jnp.float32)
        for place in range(4):
            top_rows, low_rows = [], []
            for k in range(span):
                at = ((row * 4 + place) * span + k) * span
                picks = [pick_ref[at + m] for m in range(span)]
                for entries, rows_of in ((high, top_rows), (low, low_rows)):
                    rows_of.append(
                        jnp.concatenate(
                            [
                                jnp.where(lane, entries[picks[0]], entries[picks[1]]),
                                jnp.where(lane, entries[picks[2]], entries[picks[3]]),
                            ],
                            axis=1,
                        )
                    )
            x = left_buf[place, row - begin]
            top = x.astype(jnp.bfloat16)
            rest = (x - top.astype(jnp.float32)).astype(jnp.bfloat16)
            both += jnp.dot(
                jnp.concatenate([top, rest], axis=0),
                jnp.concatenate(top_rows, axis=0),
                preferred_element_type=jnp.float32,
            )
            single += jnp.dot(
                top, jnp.concatenate(low_rows, axis=0), preferred_element_type=jnp.float32
            )
        out_ref[row - begin] = both[:width] + both[width:] + single

    @pl.loop(0, (end - begin) // ROW_STEP)
    def _(step):
        for j in range(ROW_STEP):
            one_row(begin + step * ROW_STEP + j)


def product(left, tables, picks, flags, begin, end):
    rows, width, wide = left[0].shape
    span = wide // width
    near = [pltpu.with_memory_space_constraint(x, pltpu.VMEM) for x in tables]
    return pl.pallas_call(
        functools.partial(product_kernel, begin, end, width, span),
        out_shape=jax.ShapeDtypeStruct((end - begin, width, wide), jnp.float32),
        in_specs=[pl.BlockSpec(memory_space=pltpu.SMEM)] * 2
        + [pl.BlockSpec(memory_space=pltpu.VMEM)] * len(near)
        + [pl.BlockSpec(memory_space=pl.ANY)] * len(left),
        out_specs=pl.BlockSpec(memory_space=pltpu.VMEM),
        scratch_shapes=[
            pltpu.VMEM((4, end - begin, width, wide), jnp.float32),
            pltpu.SemaphoreType.DMA((4,)),
        ],
        compiler_params=pltpu.CompilerParams(vmem_limit_bytes=PRODUCT_BYTES),
        cost_estimate=pl.CostEstimate(flops=8 * 10**9, bytes_accessed=10**7, transcendentals=0),
    )(picks, flags, *near, *left)


def spread_kernel(layers, groups, cap, wide, src, dst):
    for group in range(groups):
        for slot in range(cap):
            block = src[slot, :, group * wide : (group + 1) * wide]
            for layer in range(layers):
                dst[(layer * groups + group) * cap + slot] = block


def spread(owner_blocks, layers, groups):
    cap, width, total = owner_blocks.shape
    wide = total // groups
    return pl.pallas_call(
        functools.partial(spread_kernel, layers, groups, cap, wide),
        out_shape=jax.ShapeDtypeStruct((layers * groups * cap, width, wide), jnp.float32),
        in_specs=[pl.BlockSpec(memory_space=pltpu.VMEM)],
        out_specs=pl.BlockSpec(memory_space=pltpu.VMEM),
        compiler_params=pltpu.CompilerParams(vmem_limit_bytes=PRODUCT_BYTES),
    )(owner_blocks)


def pick_table(block_cols, out_cols, grid_row, grid_col, core, y, z, rows, span):
    cols = block_cols.reshape(N_GROUP, rows, N_GROUP, span)
    left_cols = lax.dynamic_slice(block_cols, (grid_row * rows, 0), (rows, N_GROUP * span))
    left_cols = left_cols.reshape(rows, N_GROUP, span)
    z_from = (z + jnp.array([0, 3, 1, 2], dtype=jnp.int32)) % N_Z
    groups = (core + z_from) % 2 * N_Z + z_from
    names = jnp.arange(N_GROUP, dtype=jnp.int32)
    chosen = (groups[:, None] == names[None, :]).astype(jnp.int32)
    local = left_cols - names[None, :, None] * rows
    slots = jnp.sum(local[:, None] * chosen[None, :, :, None], axis=2)
    right_cols = jnp.sum(
        cols * (names == grid_col).astype(jnp.int32)[None, None, :, None], axis=2
    )
    right_cols = jnp.sum(right_cols[None] * chosen[:, :, None, None], axis=1)
    hit = (slots[..., None] == jnp.arange(rows, dtype=jnp.int32)).astype(jnp.int32)
    found = jnp.sum(hit[..., None] * right_cols[None, :, None], axis=3)
    place = (groups // 2 - y) % N_Y
    base = ((place[None, :, None] * rows + slots) * 2)[..., None]
    match = found[..., :, None] == out_cols[:, None, None, None, :]
    piece = jnp.arange(span, dtype=jnp.int32)
    swap = (piece[:, None] + piece[None, :]) % 2
    entry = (base[..., None] + (piece // 2)[:, None]) * 2 + swap
    none = 4 * rows * span
    picked = none + jnp.sum(jnp.where(match, entry - none, 0), axis=3)
    return picked.reshape(-1).astype(jnp.int32)


def body(owner_blocks, owner_counts, block_cols, filter_mask, gamma):
    layer = lax.axis_index("layer")
    grid_row = lax.axis_index("row")
    grid_col = lax.axis_index("col")
    y, core = grid_row // N_CORE, grid_row % N_CORE
    q, z = grid_col // N_Z, grid_col % N_Z
    part = (layer + q) % 2
    cap, width, _ = owner_blocks.shape
    span = N_SLOT
    rows = block_cols.shape[0] // N_GROUP

    counts = owner_counts[0]
    ends = jnp.cumsum(counts)
    local = jnp.arange(rows, dtype=jnp.int32)
    which = jnp.sum((ends[None, :] <= local[:, None]).astype(jnp.int32), axis=1)
    slot = local - (jnp.take(ends, which) - jnp.take(counts, which))
    source = which * cap + slot
    plain_send = spread(owner_blocks, N_LAYER, N_GROUP)
    plain_got = lax.all_to_all(
        plain_send, ("layer", "col"), split_axis=0, concat_axis=0, tiled=True
    )
    row_here = 2 * y + part
    out_cols = lax.dynamic_slice(block_cols, (row_here * rows, grid_col * span), (rows, span))
    keep = lax.dynamic_slice(filter_mask, (row_here * rows, grid_col * span), (rows, span))
    picks = pick_table(block_cols, out_cols, row_here, grid_col, core, y, z, rows, span)
    flags = jnp.stack([core == (z + q) % 2, core != (part + y // 2) % 2, y >= 2]).astype(jnp.int32)

    keep_wide = jnp.repeat(keep.astype(jnp.float32), width, axis=1)[:, None, :]
    own = (out_cols == (row_here * rows + local)[:, None]).astype(jnp.float32)
    plain_got, source, picks, flags, keep_wide, own = lax.optimization_barrier(
        (plain_got, source, picks, flags, keep_wide, own)
    )
    density = plain_got.at[source].get(mode="promise_in_bounds")

    left, right = gather_first(density)
    mine = jnp.where(core == part, density, right[5])
    tables = table(right, flags)
    partial_value = product(left, tables, picks, flags, 0, rows)
    square = partial_value + swap_cores(partial_value)
    square = square * keep_wide
    unit = (own[:, None, :, None] * jnp.eye(width, dtype=jnp.float32)[None, :, None, :]).reshape(
        rows, width, span * width
    )
    mix = gamma[0]
    mixed = mix * unit + (4.0 - 2.0 * mix) * mine + (mix - 3.0) * square

    left, right = gather_second(square, mixed)
    tables = table(right, flags)

    def output(layer, y, core, q, z):
        return (1 - layer, y, core, q, z) if core == layer ^ q else None

    half = rows // 2
    totals = [product(left, tables, picks, flags, begin, begin + half) for begin in (0, half)]
    totals = [total + swap_cores(total) for total in totals]
    outs = [jnp.where(core == part, total, send(total, output)) for total in totals]
    return jnp.concatenate(outs, axis=0)


def solution(mesh):
    placed = (P(("layer", "row", "col"), None, None), P("row", None), P(), P(), P())
    return jax.shard_map(
        body, mesh=mesh, in_specs=placed, out_specs=P("row", None, "col"), check_vma=False
    )
```

```python
import functools

import jax
import jax.numpy as jnp
from jax import lax
from jax.experimental import pallas as pl
from jax.experimental.pallas import tpu as pltpu
from jax.sharding import PartitionSpec as P

AXES = ("layer", "row", "col")
N_LAYER, N_Y, N_CORE, N_Q, N_Z = 2, 4, 2, 2, 4
N_GROUP = 8
N_SLOT = 4
TABLE_STEP = 10
ROW_STEP = 5
TABLE_BYTES = 8 * 1024 * 1024
PRODUCT_BYTES = 10 * 1024 * 1024


def moves(target):
    pairs = []
    for layer in range(N_LAYER):
        for y in range(N_Y):
            for core in range(N_CORE):
                for q in range(N_Q):
                    for z in range(N_Z):
                        there = target(layer, y, core, q, z)
                        if there is not None:
                            pairs.append((flat(layer, y, core, q, z), flat(*there)))
    return pairs


def flat(layer, y, core, q, z):
    row = (y % N_Y) * N_CORE + core % N_CORE
    return ((layer % N_LAYER) * N_Y * N_CORE + row) * N_Q * N_Z + (q % N_Q) * N_Z + z % N_Z


def home_right(layer, y, core, q, z):
    return ((layer ^ q) + y // 2) % 2


def home_left(layer, y, core, q, z):
    return (z + q) % 2


def send(x, target):
    return lax.ppermute(x, AXES, moves(target))


def step(x, dy=0, dz=0):
    return send(x, lambda layer, y, core, q, z: (layer, y + dy, core, q, z + dz))


def swap_cores(x):
    return send(x, lambda layer, y, core, q, z: (layer, y, 1 - core, q, z))


def after(x, *done):
    return lax.optimization_barrier((x, *done))[0]


def left_pass(layer, y, core, q, z):
    return (1 - layer, y, core, 1 - q, z) if core == home_left(layer, y, core, q, z) else None


def gather_first(density):
    def right_step(dy):
        return lambda layer, y, core, q, z: (layer, y + dy, core + y // 2, q, z)

    def left_own(layer, y, core, q, z):
        if core == layer ^ q:
            return layer, y, z + q, q, z
        return layer, y, z + q, 1 - q, z

    def left_across(layer, y, core, q, z):
        return (layer, y, z + q, q, z + 2) if core == layer ^ q else None

    half = density.shape[0] // 2
    below = send(density, right_step(1))
    above = send(density, right_step(-1))
    left = send(density, left_own)
    across = send(density, left_across)
    swapped = swap_cores(density)
    left_now = after(left, across, swapped)
    left_below = step(left_now, dz=1)
    left_above = step(left_now, dz=-1)
    left_pair = send(across, left_pass)
    first = step(below[:half], dy=1)
    second = step(above[half:], dy=-1)
    return (left, left_below, left_above, across, left_pair), (density, above, first, below, second, swapped)


def gather_second(square, mixed):
    def right_own(layer, y, core, q, z):
        home = home_right(layer, y, core, q, z)
        return (1 - layer, y, core, q, z) if core == home else (layer, y, home, q, z)

    def left_own(layer, y, core, q, z):
        home = home_left(layer, y, core, q, z)
        return (1 - layer, y, core, 1 - q, z) if core == home else (layer, y, home, q, z)

    def right_across(layer, y, core, q, z):
        return (layer, y + 2, core, q, z) if core == home_right(layer, y, core, q, z) else None

    def left_across(layer, y, core, q, z):
        return (layer, y, core, q, z + 2) if core == home_left(layer, y, core, q, z) else None

    def right_pass(layer, y, core, q, z):
        return (1 - layer, y, core, q, z) if core != home_right(layer, y, core, q, z) else None

    own = send(mixed, right_own)
    left = send(square, left_own)
    across = send(mixed, right_across)
    left_across = send(square, left_across)
    left_now = after(left, own)
    below = step(own, dy=1)
    above = step(own, dy=-1)
    left_below = step(left_now, dz=1)
    left_above = step(left_now, dz=-1)
    pair = send(after(across, own), right_pass)
    left_pair = send(after(left_across, pair), left_pass)
    return (left, left_below, left_above, left_across, left_pair), (own, above, across, below, pair)


def table_kernel(rows, width, span, jobs, count, fresh, flag_ref, *refs):
    source = refs[:count]
    high, low, buf, sem = refs[-4:]
    half = rows // 2
    starts = []
    for job, (place, names, flag) in enumerate(jobs):
        whole = pltpu.make_async_copy(source[names[0]], buf.at[job], sem.at[job, 0])
        if len(names) == 1:
            whole.start()
            starts.append([whole])
        elif flag is None:
            parts = [
                pltpu.make_async_copy(
                    source[name], buf.at[job, pl.ds(part * half, half)], sem.at[job, part]
                )
                for part, name in enumerate(names)
            ]
            for copy in parts:
                copy.start()
            starts.append(parts)
        else:

            @pl.when(flag_ref[flag] == 1)
            def _():
                whole.start()

            @pl.when(flag_ref[flag] == 0)
            def _():
                pltpu.make_async_copy(source[names[1]], buf.at[job], sem.at[job, 0]).start()

            starts.append([whole])

    if fresh:
        none = 4 * rows * span
        high[none] = jnp.zeros(high.shape[1:], high.dtype)
        low[none] = jnp.zeros(low.shape[1:], low.dtype)

    for job, (place, names, flag) in enumerate(jobs):
        for copy in starts[job]:
            copy.wait()

        @pl.loop(0, rows // TABLE_STEP)
        def _(step):
            for j in range(TABLE_STEP):
                row = step * TABLE_STEP + j
                at = (place * rows + row) * span
                x = buf[job, row]
                for v in range(2):
                    piece = x[:, v * 2 * width : (v + 1) * 2 * width]
                    for swap, part in enumerate((piece, pltpu.roll(piece, width, 1))):
                        top = part.astype(jnp.bfloat16)
                        high[at + 2 * v + swap] = top
                        low[at + 2 * v + swap] = (part - top.astype(jnp.float32)).astype(jnp.bfloat16)


def table(panels, jobs, flags, rows, before=()):
    width, wide = panels[0].shape[1:]
    span = wide // width
    count = len(panels)
    kind = pltpu.VMEM((4 * rows * span + 1, width, 2 * width), jnp.bfloat16)
    near = [pltpu.with_memory_space_constraint(x, pltpu.VMEM) for x in before]
    return pl.pallas_call(
        functools.partial(table_kernel, rows, width, span, jobs, count, not before),
        out_shape=(kind, kind),
        in_specs=[pl.BlockSpec(memory_space=pltpu.SMEM)]
        + [pl.BlockSpec(memory_space=pl.ANY)] * count
        + [pl.BlockSpec(memory_space=pltpu.VMEM)] * len(before),
        out_specs=(pl.BlockSpec(memory_space=pltpu.VMEM),) * 2,
        scratch_shapes=[
            pltpu.VMEM((len(jobs), rows, width, wide), jnp.float32),
            pltpu.SemaphoreType.DMA((len(jobs), 2)),
        ],
        input_output_aliases={1 + count + i: i for i in range(len(before))},
        compiler_params=pltpu.CompilerParams(vmem_limit_bytes=TABLE_BYTES),
        cost_estimate=pl.CostEstimate(flops=2 * 10**9, bytes_accessed=10**7, transcendentals=0),
    )(flags, *panels, *near)


def product_kernel(first, begin, end, width, span, pick_ref, flag_ref, high, low, *refs):
    left = refs[:5]
    out_ref, left_buf, left_sem = refs[5:]

    def bring(place, src):
        rows_here = src.at[pl.ds(begin, end - begin)]
        return pltpu.make_async_copy(rows_here, left_buf.at[place - first], left_sem.at[place - first])

    for place in range(first, 3):
        bring(place, left[place]).start()

    @pl.when(flag_ref[0] == 1)
    def _():
        bring(3, left[3]).start()

    @pl.when(flag_ref[0] == 0)
    def _():
        bring(3, left[4]).start()

    for place in range(first, 4):
        bring(place, left[3]).wait()

    lane = lax.broadcasted_iota(jnp.int32, (width, 2 * width), 1) < width

    def one_row(row):
        both = jnp.zeros((2 * width, span * width), jnp.float32)
        single = jnp.zeros((width, span * width), jnp.float32)
        for place in range(4):
            top_rows, low_rows = [], []
            for k in range(span):
                at = ((row * 4 + place) * span + k) * span
                picks = [pick_ref[at + m] for m in range(span)]
                for entries, rows_of in ((high, top_rows), (low, low_rows)):
                    rows_of.append(
                        jnp.concatenate(
                            [
                                jnp.where(lane, entries[picks[0]], entries[picks[1]]),
                                jnp.where(lane, entries[picks[2]], entries[picks[3]]),
                            ],
                            axis=1,
                        )
                    )
            x = left[place][row] if place < first else left_buf[place - first, row - begin]
            top = x.astype(jnp.bfloat16)
            rest = (x - top.astype(jnp.float32)).astype(jnp.bfloat16)
            both += jnp.dot(
                jnp.concatenate([top, rest], axis=0),
                jnp.concatenate(top_rows, axis=0),
                preferred_element_type=jnp.float32,
            )
            single += jnp.dot(
                top, jnp.concatenate(low_rows, axis=0), preferred_element_type=jnp.float32
            )
        out_ref[row - begin] = both[:width] + both[width:] + single

    @pl.loop(0, (end - begin) // ROW_STEP)
    def _(step):
        for j in range(ROW_STEP):
            one_row(begin + step * ROW_STEP + j)


def product(left, tables, picks, flags, begin, end, first=0):
    rows, width, wide = left[0].shape
    span = wide // width
    near = [pltpu.with_memory_space_constraint(x, pltpu.VMEM) for x in (*tables, *left[:first])]
    return pl.pallas_call(
        functools.partial(product_kernel, first, begin, end, width, span),
        out_shape=jax.ShapeDtypeStruct((end - begin, width, wide), jnp.float32),
        in_specs=[pl.BlockSpec(memory_space=pltpu.SMEM)] * 2
        + [pl.BlockSpec(memory_space=pltpu.VMEM)] * len(near)
        + [pl.BlockSpec(memory_space=pl.ANY)] * (5 - first),
        out_specs=pl.BlockSpec(memory_space=pltpu.VMEM),
        scratch_shapes=[
            pltpu.VMEM((4 - first, end - begin, width, wide), jnp.float32),
            pltpu.SemaphoreType.DMA((4 - first,)),
        ],
        compiler_params=pltpu.CompilerParams(vmem_limit_bytes=PRODUCT_BYTES),
        cost_estimate=pl.CostEstimate(flops=8 * 10**9, bytes_accessed=10**7, transcendentals=0),
    )(picks, flags, *near, *left[first:])


def spread_kernel(layers, groups, cap, wide, src, dst):
    for group in range(groups):
        for slot in range(cap):
            block = src[slot, :, group * wide : (group + 1) * wide]
            for layer in range(layers):
                dst[(layer * groups + group) * cap + slot] = block


def spread(owner_blocks, layers, groups):
    cap, width, total = owner_blocks.shape
    wide = total // groups
    return pl.pallas_call(
        functools.partial(spread_kernel, layers, groups, cap, wide),
        out_shape=jax.ShapeDtypeStruct((layers * groups * cap, width, wide), jnp.float32),
        in_specs=[pl.BlockSpec(memory_space=pltpu.VMEM)],
        out_specs=pl.BlockSpec(memory_space=pltpu.VMEM),
        compiler_params=pltpu.CompilerParams(vmem_limit_bytes=PRODUCT_BYTES),
    )(owner_blocks)


def pick_table(block_cols, out_cols, grid_row, grid_col, core, y, z, rows, span):
    cols = block_cols.reshape(N_GROUP, rows, N_GROUP, span)
    left_cols = lax.dynamic_slice(block_cols, (grid_row * rows, 0), (rows, N_GROUP * span))
    left_cols = left_cols.reshape(rows, N_GROUP, span)
    z_from = (z + jnp.array([0, 3, 1, 2], dtype=jnp.int32)) % N_Z
    groups = (core + z_from) % 2 * N_Z + z_from
    names = jnp.arange(N_GROUP, dtype=jnp.int32)
    chosen = (groups[:, None] == names[None, :]).astype(jnp.int32)
    local = left_cols - names[None, :, None] * rows
    slots = jnp.sum(local[:, None] * chosen[None, :, :, None], axis=2)
    right_cols = jnp.sum(
        cols * (names == grid_col).astype(jnp.int32)[None, None, :, None], axis=2
    )
    right_cols = jnp.sum(right_cols[None] * chosen[:, :, None, None], axis=1)
    hit = (slots[..., None] == jnp.arange(rows, dtype=jnp.int32)).astype(jnp.int32)
    found = jnp.sum(hit[..., None] * right_cols[None, :, None], axis=3)
    place = (groups // 2 - y) % N_Y
    base = ((place[None, :, None] * rows + slots) * 2)[..., None]
    match = found[..., :, None] == out_cols[:, None, None, None, :]
    piece = jnp.arange(span, dtype=jnp.int32)
    swap = (piece[:, None] + piece[None, :]) % 2
    entry = (base[..., None] + (piece // 2)[:, None]) * 2 + swap
    none = 4 * rows * span
    picked = none + jnp.sum(jnp.where(match, entry - none, 0), axis=3)
    return picked.reshape(-1).astype(jnp.int32)


def body(owner_blocks, owner_counts, block_cols, filter_mask, gamma):
    layer = lax.axis_index("layer")
    grid_row = lax.axis_index("row")
    grid_col = lax.axis_index("col")
    y, core = grid_row // N_CORE, grid_row % N_CORE
    q, z = grid_col // N_Z, grid_col % N_Z
    part = (layer + q) % 2
    cap, width, _ = owner_blocks.shape
    span = N_SLOT
    rows = block_cols.shape[0] // N_GROUP

    counts = owner_counts[0]
    ends = jnp.cumsum(counts)
    local = jnp.arange(rows, dtype=jnp.int32)
    which = jnp.sum((ends[None, :] <= local[:, None]).astype(jnp.int32), axis=1)
    slot = local - (jnp.take(ends, which) - jnp.take(counts, which))
    source = which * cap + slot
    plain_send = spread(owner_blocks, N_LAYER, N_GROUP)
    plain_got = lax.all_to_all(
        plain_send, ("layer", "col"), split_axis=0, concat_axis=0, tiled=True
    )
    row_here = 2 * y + part
    out_cols = lax.dynamic_slice(block_cols, (row_here * rows, grid_col * span), (rows, span))
    keep = lax.dynamic_slice(filter_mask, (row_here * rows, grid_col * span), (rows, span))
    picks = pick_table(block_cols, out_cols, row_here, grid_col, core, y, z, rows, span)
    flags = jnp.stack([core == (z + q) % 2, core != (part + y // 2) % 2, y >= 2]).astype(jnp.int32)

    keep_wide = jnp.repeat(keep.astype(jnp.float32), width, axis=1)[:, None, :]
    own = (out_cols == (row_here * rows + local)[:, None]).astype(jnp.float32)
    plain_got, source, picks, flags, keep_wide, own = lax.optimization_barrier(
        (plain_got, source, picks, flags, keep_wide, own)
    )
    density = plain_got.at[source].get(mode="promise_in_bounds")

    left, right = gather_first(density)
    mine = jnp.where(core == part, density, right[5])
    density, above, first, below, second, swapped = right
    jobs = ((0, (0, 1), 2), (1, (2,), None), (3, (3,), None))
    tables = table((swapped, density, above, below), jobs, flags, rows)
    tables = table((first, second), ((2, (0, 1), None),), flags, rows, tables)
    partial_value = product(left, tables, picks, flags, 0, rows)
    square = partial_value + swap_cores(partial_value)
    square = square * keep_wide
    unit = (own[:, None, :, None] * jnp.eye(width, dtype=jnp.float32)[None, :, None, :]).reshape(
        rows, width, span * width
    )
    mix = gamma[0]
    mixed = mix * unit + (4.0 - 2.0 * mix) * mine + (mix - 3.0) * square

    left, right = gather_second(square, mixed)
    own_right, above, across, below, pair = right
    jobs = ((0, (0,), None), (2, (1, 2), 1))
    tables = table((own_right, across, pair), jobs, flags, rows)
    tables = table((above, below), ((1, (0,), None), (3, (1,), None)), flags, rows, tables)

    def output(layer, y, core, q, z):
        return (1 - layer, y, core, q, z) if core == layer ^ q else None

    half = rows // 2
    totals = [product(left, tables, picks, flags, begin, begin + half, 3) for begin in (0, half)]
    totals = [total + swap_cores(total) for total in totals]
    outs = [jnp.where(core == part, total, send(total, output)) for total in totals]
    return jnp.concatenate(outs, axis=0)


def solution(mesh):
    placed = (P(("layer", "row", "col"), None, None), P("row", None), P(), P(), P())
    return jax.shard_map(
        body, mesh=mesh, in_specs=placed, out_specs=P("row", None, "col"), check_vma=False
    )
```

```python
import functools

import jax
import jax.numpy as jnp
from jax import lax
from jax.experimental import pallas as pl
from jax.experimental.pallas import tpu as pltpu
from jax.sharding import PartitionSpec as P

AXES = ("layer", "row", "col")
N_LAYER, N_Y, N_CORE, N_Q, N_Z = 2, 4, 2, 2, 4
N_GROUP = 8
N_SLOT = 4
TABLE_STEP = 10
ROW_STEP = 5
SPREAD_BYTES = 4 * 1024 * 1024
TABLE_BYTES = 5 * 1024 * 1024
PRODUCT_BYTES = 7 * 1024 * 1024


def moves(target):
    pairs = []
    for layer in range(N_LAYER):
        for y in range(N_Y):
            for core in range(N_CORE):
                for q in range(N_Q):
                    for z in range(N_Z):
                        there = target(layer, y, core, q, z)
                        if there is not None:
                            pairs.append((flat(layer, y, core, q, z), flat(*there)))
    return pairs


def flat(layer, y, core, q, z):
    row = (y % N_Y) * N_CORE + core % N_CORE
    return ((layer % N_LAYER) * N_Y * N_CORE + row) * N_Q * N_Z + (q % N_Q) * N_Z + z % N_Z


def home_right(layer, y, core, q, z):
    return ((layer ^ q) + y // 2) % 2


def home_left(layer, y, core, q, z):
    return (z + q) % 2


def send(x, target):
    return lax.ppermute(x, AXES, moves(target))


def step(x, dy=0, dz=0):
    return send(x, lambda layer, y, core, q, z: (layer, y + dy, core, q, z + dz))


def swap_cores(x):
    return send(x, lambda layer, y, core, q, z: (layer, y, 1 - core, q, z))


def after(x, *done):
    return lax.optimization_barrier((x, *done))[0]


def left_pass(layer, y, core, q, z):
    return (1 - layer, y, core, 1 - q, z) if core == home_left(layer, y, core, q, z) else None


def gather_first(density):
    def right_step(dy):
        return lambda layer, y, core, q, z: (layer, y + dy, core + y // 2, q, z)

    def left_own(layer, y, core, q, z):
        if core == layer ^ q:
            return layer, y, z + q, q, z
        return layer, y, z + q, 1 - q, z

    def left_across(layer, y, core, q, z):
        return (layer, y, z + q, q, z + 2) if core == layer ^ q else None

    half = density.shape[0] // 2
    below = send(density, right_step(1))
    above = send(density, right_step(-1))
    left = send(density, left_own)
    across = send(density, left_across)
    swapped = swap_cores(density)
    left_now = after(left, swapped)
    left_below = step(left_now, dz=1)
    left_above = step(left_now, dz=-1)
    left_pair = send(across, left_pass)
    first = step(below[:half], dy=1)
    second = step(above[half:], dy=-1)
    return (left, left_below, left_above, across, left_pair), (density, above, first, below, second, swapped)


def gather_second(square, mixed):
    def right_own(layer, y, core, q, z):
        home = home_right(layer, y, core, q, z)
        return (1 - layer, y, core, q, z) if core == home else (layer, y, home, q, z)

    def left_own(layer, y, core, q, z):
        home = home_left(layer, y, core, q, z)
        return (1 - layer, y, core, 1 - q, z) if core == home else (layer, y, home, q, z)

    def right_across(layer, y, core, q, z):
        return (layer, y + 2, core, q, z) if core == home_right(layer, y, core, q, z) else None

    def left_across(layer, y, core, q, z):
        return (layer, y, core, q, z + 2) if core == home_left(layer, y, core, q, z) else None

    def right_pass(layer, y, core, q, z):
        return (1 - layer, y, core, q, z) if core != home_right(layer, y, core, q, z) else None

    own = send(mixed, right_own)
    left = send(square, left_own)
    across = send(mixed, right_across)
    left_across = send(square, left_across)
    left_now = after(left, own)
    below = step(own, dy=1)
    above = step(own, dy=-1)
    left_below = step(left_now, dz=1)
    left_above = step(left_now, dz=-1)
    pair = send(after(across, own), right_pass)
    left_pair = send(after(left_across, pair), left_pass)
    return (left, left_below, left_above, left_across, left_pair), (own, above, across, below, pair)


def table_kernel(rows, width, span, jobs, count, fresh, flag_ref, *refs):
    source = refs[:count]
    high, low, buf, sem = refs[-4:]
    half = rows // 2
    starts = []
    for job, (place, names, flag) in enumerate(jobs):
        whole = pltpu.make_async_copy(source[names[0]], buf.at[job], sem.at[job, 0])
        if len(names) == 1:
            whole.start()
            starts.append([whole])
        elif flag is None:
            parts = [
                pltpu.make_async_copy(
                    source[name], buf.at[job, pl.ds(part * half, half)], sem.at[job, part]
                )
                for part, name in enumerate(names)
            ]
            for copy in parts:
                copy.start()
            starts.append(parts)
        else:

            @pl.when(flag_ref[flag] == 1)
            def _():
                whole.start()

            @pl.when(flag_ref[flag] == 0)
            def _():
                pltpu.make_async_copy(source[names[1]], buf.at[job], sem.at[job, 0]).start()

            starts.append([whole])

    if fresh:
        none = 4 * rows * span
        high[none] = jnp.zeros(high.shape[1:], high.dtype)
        low[none] = jnp.zeros(low.shape[1:], low.dtype)

    for job, (place, names, flag) in enumerate(jobs):
        for copy in starts[job]:
            copy.wait()

        @pl.loop(0, rows // TABLE_STEP)
        def _(step):
            for j in range(TABLE_STEP):
                row = step * TABLE_STEP + j
                at = (place * rows + row) * span
                x = buf[job, row]
                for v in range(2):
                    piece = x[:, v * 2 * width : (v + 1) * 2 * width]
                    for swap, part in enumerate((piece, pltpu.roll(piece, width, 1))):
                        top = part.astype(jnp.bfloat16)
                        high[at + 2 * v + swap] = top
                        low[at + 2 * v + swap] = (part - top.astype(jnp.float32)).astype(jnp.bfloat16)


def table(panels, jobs, flags, rows, before=()):
    width, wide = panels[0].shape[1:]
    span = wide // width
    count = len(panels)
    kind = pltpu.VMEM((4 * rows * span + 1, width, 2 * width), jnp.bfloat16)
    near = [pltpu.with_memory_space_constraint(x, pltpu.VMEM) for x in before]
    return pl.pallas_call(
        functools.partial(table_kernel, rows, width, span, jobs, count, not before),
        out_shape=(kind, kind),
        in_specs=[pl.BlockSpec(memory_space=pltpu.SMEM)]
        + [pl.BlockSpec(memory_space=pl.ANY)] * count
        + [pl.BlockSpec(memory_space=pltpu.VMEM)] * len(before),
        out_specs=(pl.BlockSpec(memory_space=pltpu.VMEM),) * 2,
        scratch_shapes=[
            pltpu.VMEM((len(jobs), rows, width, wide), jnp.float32),
            pltpu.SemaphoreType.DMA((len(jobs), 2)),
        ],
        input_output_aliases={1 + count + i: i for i in range(len(before))},
        compiler_params=pltpu.CompilerParams(vmem_limit_bytes=TABLE_BYTES),
        cost_estimate=pl.CostEstimate(flops=2 * 10**9, bytes_accessed=10**7, transcendentals=0),
    )(flags, *panels, *near)


def product_kernel(first, begin, end, width, span, pick_ref, flag_ref, high, low, *refs):
    left = refs[:5]
    out_ref, left_buf, left_sem = refs[5:]

    def bring(place, src):
        rows_here = src.at[pl.ds(begin, end - begin)]
        return pltpu.make_async_copy(rows_here, left_buf.at[place - first], left_sem.at[place - first])

    for place in range(first, 3):
        bring(place, left[place]).start()

    @pl.when(flag_ref[0] == 1)
    def _():
        bring(3, left[3]).start()

    @pl.when(flag_ref[0] == 0)
    def _():
        bring(3, left[4]).start()

    for place in range(first, 4):
        bring(place, left[3]).wait()

    lane = lax.broadcasted_iota(jnp.int32, (width, 2 * width), 1) < width

    def one_row(row):
        both = jnp.zeros((2 * width, span * width), jnp.float32)
        single = jnp.zeros((width, span * width), jnp.float32)
        for place in range(4):
            top_rows, low_rows = [], []
            for k in range(span):
                at = ((row * 4 + place) * span + k) * span
                picks = [pick_ref[at + m] for m in range(span)]
                for entries, rows_of in ((high, top_rows), (low, low_rows)):
                    rows_of.append(
                        jnp.concatenate(
                            [
                                jnp.where(lane, entries[picks[0]], entries[picks[1]]),
                                jnp.where(lane, entries[picks[2]], entries[picks[3]]),
                            ],
                            axis=1,
                        )
                    )
            x = left[place][row] if place < first else left_buf[place - first, row - begin]
            top = x.astype(jnp.bfloat16)
            rest = (x - top.astype(jnp.float32)).astype(jnp.bfloat16)
            both += jnp.dot(
                jnp.concatenate([top, rest], axis=0),
                jnp.concatenate(top_rows, axis=0),
                preferred_element_type=jnp.float32,
            )
            single += jnp.dot(
                top, jnp.concatenate(low_rows, axis=0), preferred_element_type=jnp.float32
            )
        out_ref[row - begin] = both[:width] + both[width:] + single

    @pl.loop(0, (end - begin) // ROW_STEP)
    def _(step):
        for j in range(ROW_STEP):
            one_row(begin + step * ROW_STEP + j)


def product(left, tables, picks, flags, begin, end, first=0):
    rows, width, wide = left[0].shape
    span = wide // width
    near = [pltpu.with_memory_space_constraint(x, pltpu.VMEM) for x in (*tables, *left[:first])]
    return pl.pallas_call(
        functools.partial(product_kernel, first, begin, end, width, span),
        out_shape=jax.ShapeDtypeStruct((end - begin, width, wide), jnp.float32),
        in_specs=[pl.BlockSpec(memory_space=pltpu.SMEM)] * 2
        + [pl.BlockSpec(memory_space=pltpu.VMEM)] * len(near)
        + [pl.BlockSpec(memory_space=pl.ANY)] * (5 - first),
        out_specs=pl.BlockSpec(memory_space=pltpu.VMEM),
        scratch_shapes=[
            pltpu.VMEM((4 - first, end - begin, width, wide), jnp.float32),
            pltpu.SemaphoreType.DMA((4 - first,)),
        ],
        compiler_params=pltpu.CompilerParams(vmem_limit_bytes=PRODUCT_BYTES),
        cost_estimate=pl.CostEstimate(flops=8 * 10**9, bytes_accessed=10**7, transcendentals=0),
    )(picks, flags, *near, *left[first:])


def spread_kernel(layers, groups, cap, wide, src, dst):
    for group in range(groups):
        for slot in range(cap):
            block = src[slot, :, group * wide : (group + 1) * wide]
            for layer in range(layers):
                dst[(layer * groups + group) * cap + slot] = block


def spread(owner_blocks, layers, groups):
    cap, width, total = owner_blocks.shape
    wide = total // groups
    return pl.pallas_call(
        functools.partial(spread_kernel, layers, groups, cap, wide),
        out_shape=jax.ShapeDtypeStruct((layers * groups * cap, width, wide), jnp.float32),
        in_specs=[pl.BlockSpec(memory_space=pltpu.VMEM)],
        out_specs=pl.BlockSpec(memory_space=pltpu.VMEM),
        compiler_params=pltpu.CompilerParams(vmem_limit_bytes=SPREAD_BYTES),
    )(owner_blocks)


def pick_table(block_cols, out_cols, grid_row, grid_col, core, y, z, rows, span):
    cols = block_cols.reshape(N_GROUP, rows, N_GROUP, span)
    left_cols = lax.dynamic_slice(block_cols, (grid_row * rows, 0), (rows, N_GROUP * span))
    left_cols = left_cols.reshape(rows, N_GROUP, span)
    z_from = (z + jnp.array([0, 3, 1, 2], dtype=jnp.int32)) % N_Z
    groups = (core + z_from) % 2 * N_Z + z_from
    names = jnp.arange(N_GROUP, dtype=jnp.int32)
    chosen = (groups[:, None] == names[None, :]).astype(jnp.int32)
    local = left_cols - names[None, :, None] * rows
    slots = jnp.sum(local[:, None] * chosen[None, :, :, None], axis=2)
    right_cols = jnp.sum(
        cols * (names == grid_col).astype(jnp.int32)[None, None, :, None], axis=2
    )
    right_cols = jnp.sum(right_cols[None] * chosen[:, :, None, None], axis=1)
    hit = (slots[..., None] == jnp.arange(rows, dtype=jnp.int32)).astype(jnp.int32)
    found = jnp.sum(hit[..., None] * right_cols[None, :, None], axis=3)
    place = (groups // 2 - y) % N_Y
    base = ((place[None, :, None] * rows + slots) * 2)[..., None]
    match = found[..., :, None] == out_cols[:, None, None, None, :]
    piece = jnp.arange(span, dtype=jnp.int32)
    swap = (piece[:, None] + piece[None, :]) % 2
    entry = (base[..., None] + (piece // 2)[:, None]) * 2 + swap
    none = 4 * rows * span
    picked = none + jnp.sum(jnp.where(match, entry - none, 0), axis=3)
    return picked.reshape(-1).astype(jnp.int32)


def body(owner_blocks, owner_counts, block_cols, filter_mask, gamma):
    layer = lax.axis_index("layer")
    grid_row = lax.axis_index("row")
    grid_col = lax.axis_index("col")
    y, core = grid_row // N_CORE, grid_row % N_CORE
    q, z = grid_col // N_Z, grid_col % N_Z
    part = (layer + q) % 2
    cap, width, _ = owner_blocks.shape
    span = N_SLOT
    rows = block_cols.shape[0] // N_GROUP

    counts = owner_counts[0]
    ends = jnp.cumsum(counts)
    local = jnp.arange(rows, dtype=jnp.int32)
    which = jnp.sum((ends[None, :] <= local[:, None]).astype(jnp.int32), axis=1)
    slot = local - (jnp.take(ends, which) - jnp.take(counts, which))
    source = which * cap + slot
    plain_send = spread(owner_blocks, N_LAYER, N_GROUP)
    plain_got = lax.all_to_all(
        plain_send, ("layer", "col"), split_axis=0, concat_axis=0, tiled=True
    )
    row_here = 2 * y + part
    out_cols = lax.dynamic_slice(block_cols, (row_here * rows, grid_col * span), (rows, span))
    keep = lax.dynamic_slice(filter_mask, (row_here * rows, grid_col * span), (rows, span))
    picks = pick_table(block_cols, out_cols, row_here, grid_col, core, y, z, rows, span)
    flags = jnp.stack([core == (z + q) % 2, core != (part + y // 2) % 2, y >= 2]).astype(jnp.int32)

    keep_wide = jnp.repeat(keep.astype(jnp.float32), width, axis=1)[:, None, :]
    own = (out_cols == (row_here * rows + local)[:, None]).astype(jnp.float32)
    plain_got, source, picks, flags, keep_wide, own = lax.optimization_barrier(
        (plain_got, source, picks, flags, keep_wide, own)
    )
    density = plain_got.at[source].get(mode="promise_in_bounds")

    left, right = gather_first(density)
    mine = jnp.where(core == part, density, right[5])
    density, above, first, below, second, swapped = right
    jobs = ((0, (0, 1), 2), (1, (2,), None), (3, (3,), None))
    tables = table((swapped, density, above, below), jobs, flags, rows)
    tables = table((first, second), ((2, (0, 1), None),), flags, rows, tables)
    partial_value = product(left, tables, picks, flags, 0, rows, 3)
    square = partial_value + swap_cores(partial_value)
    square = square * keep_wide
    unit = (own[:, None, :, None] * jnp.eye(width, dtype=jnp.float32)[None, :, None, :]).reshape(
        rows, width, span * width
    )
    mix = gamma[0]
    mixed = mix * unit + (4.0 - 2.0 * mix) * mine + (mix - 3.0) * square

    left, right = gather_second(square, mixed)
    own_right, above, across, below, pair = right
    jobs = ((0, (0,), None), (2, (1, 2), 1))
    tables = table((own_right, across, pair), jobs, flags, rows)
    tables = table((above, below), ((1, (0,), None), (3, (1,), None)), flags, rows, tables)

    def output(layer, y, core, q, z):
        return (1 - layer, y, core, q, z) if core == layer ^ q else None

    half = rows // 2
    totals = [product(left, tables, picks, flags, begin, begin + half, 3) for begin in (0, half)]
    totals = [total + swap_cores(total) for total in totals]
    outs = [jnp.where(core == part, total, send(total, output)) for total in totals]
    return jnp.concatenate(outs, axis=0)


def solution(mesh):
    placed = (P(("layer", "row", "col"), None, None), P("row", None), P(), P(), P())
    return jax.shard_map(
        body, mesh=mesh, in_specs=placed, out_specs=P("row", None, "col"), check_vma=False
    )
```

```python
import functools

import jax
import jax.numpy as jnp
from jax import lax
from jax.experimental import pallas as pl
from jax.experimental.pallas import tpu as pltpu
from jax.sharding import PartitionSpec as P

AXES = ("layer", "row", "col")
N_LAYER, N_Y, N_CORE, N_Q, N_Z = 2, 4, 2, 2, 4
N_GROUP = 8
N_SLOT = 4
TABLE_STEP = 10
ROW_STEP = 5
SPREAD_BYTES = 4 * 1024 * 1024
TABLE_BYTES = 5 * 1024 * 1024
PRODUCT_BYTES = 7 * 1024 * 1024


def moves(target):
    pairs = []
    for layer in range(N_LAYER):
        for y in range(N_Y):
            for core in range(N_CORE):
                for q in range(N_Q):
                    for z in range(N_Z):
                        there = target(layer, y, core, q, z)
                        if there is not None:
                            pairs.append((flat(layer, y, core, q, z), flat(*there)))
    return pairs


def flat(layer, y, core, q, z):
    row = (y % N_Y) * N_CORE + core % N_CORE
    return ((layer % N_LAYER) * N_Y * N_CORE + row) * N_Q * N_Z + (q % N_Q) * N_Z + z % N_Z


def home_right(layer, y, core, q, z):
    return ((layer ^ q) + y // 2) % 2


def home_left(layer, y, core, q, z):
    return (z + q) % 2


def send(x, target):
    return lax.ppermute(x, AXES, moves(target))


def step(x, dy=0, dz=0):
    return send(x, lambda layer, y, core, q, z: (layer, y + dy, core, q, z + dz))


def swap_cores(x):
    return send(x, lambda layer, y, core, q, z: (layer, y, 1 - core, q, z))


def after(x, *done):
    return lax.optimization_barrier((x, *done))[0]


def left_pass(layer, y, core, q, z):
    return (1 - layer, y, core, 1 - q, z) if core == home_left(layer, y, core, q, z) else None


def gather_first(density):
    def right_step(dy):
        return lambda layer, y, core, q, z: (layer, y + dy, core + y // 2, q, z)

    def left_own(layer, y, core, q, z):
        if core == layer ^ q:
            return layer, y, z + q, q, z
        return layer, y, z + q, 1 - q, z

    def left_across(layer, y, core, q, z):
        return (layer, y, z + q, q, z + 2) if core == layer ^ q else None

    half = density.shape[0] // 2
    below = send(density, right_step(1))
    above = send(density, right_step(-1))
    left = send(density, left_own)
    across = send(density, left_across)
    swapped = swap_cores(density)
    left_now = after(left, swapped)
    left_below = step(left_now, dz=1)
    left_above = step(left_now, dz=-1)
    first = step(below[:half], dy=1)
    second = step(above[half:], dy=-1)
    left_pair = send(after(across, below, above), left_pass)
    return (left, left_below, left_above, across, left_pair), (density, above, first, below, second, swapped)


def gather_second(square, mixed):
    def right_own(layer, y, core, q, z):
        home = home_right(layer, y, core, q, z)
        return (1 - layer, y, core, q, z) if core == home else (layer, y, home, q, z)

    def left_own(layer, y, core, q, z):
        home = home_left(layer, y, core, q, z)
        return (1 - layer, y, core, 1 - q, z) if core == home else (layer, y, home, q, z)

    def right_across(layer, y, core, q, z):
        return (layer, y + 2, core, q, z) if core == home_right(layer, y, core, q, z) else None

    def left_across(layer, y, core, q, z):
        return (layer, y, core, q, z + 2) if core == home_left(layer, y, core, q, z) else None

    def right_pass(layer, y, core, q, z):
        return (1 - layer, y, core, q, z) if core != home_right(layer, y, core, q, z) else None

    own = send(mixed, right_own)
    left = send(square, left_own)
    across = send(mixed, right_across)
    left_across = send(square, left_across)
    left_now = after(left, own)
    below = step(own, dy=1)
    above = step(own, dy=-1)
    left_below = step(left_now, dz=1)
    left_above = step(left_now, dz=-1)
    pair = send(after(across, own), right_pass)
    left_pair = send(after(left_across, pair), left_pass)
    return (left, left_below, left_above, left_across, left_pair), (own, above, across, below, pair)


def table_kernel(rows, width, span, jobs, count, fresh, flag_ref, *refs):
    source = refs[:count]
    high, low, buf, sem = refs[-4:]
    half = rows // 2
    starts = []
    for job, (place, names, flag) in enumerate(jobs):
        whole = pltpu.make_async_copy(source[names[0]], buf.at[job], sem.at[job, 0])
        if len(names) == 1:
            whole.start()
            starts.append([whole])
        elif flag is None:
            parts = [
                pltpu.make_async_copy(
                    source[name], buf.at[job, pl.ds(part * half, half)], sem.at[job, part]
                )
                for part, name in enumerate(names)
            ]
            for copy in parts:
                copy.start()
            starts.append(parts)
        else:

            @pl.when(flag_ref[flag] == 1)
            def _():
                whole.start()

            @pl.when(flag_ref[flag] == 0)
            def _():
                pltpu.make_async_copy(source[names[1]], buf.at[job], sem.at[job, 0]).start()

            starts.append([whole])

    if fresh:
        none = 4 * rows * span
        high[none] = jnp.zeros(high.shape[1:], high.dtype)
        low[none] = jnp.zeros(low.shape[1:], low.dtype)

    for job, (place, names, flag) in enumerate(jobs):
        for copy in starts[job]:
            copy.wait()

        @pl.loop(0, rows // TABLE_STEP)
        def _(step):
            for j in range(TABLE_STEP):
                row = step * TABLE_STEP + j
                at = (place * rows + row) * span
                x = buf[job, row]
                for v in range(2):
                    piece = x[:, v * 2 * width : (v + 1) * 2 * width]
                    for swap, part in enumerate((piece, pltpu.roll(piece, width, 1))):
                        top = part.astype(jnp.bfloat16)
                        high[at + 2 * v + swap] = top
                        low[at + 2 * v + swap] = (part - top.astype(jnp.float32)).astype(jnp.bfloat16)


def table(panels, jobs, flags, rows, before=()):
    width, wide = panels[0].shape[1:]
    span = wide // width
    count = len(panels)
    kind = pltpu.VMEM((4 * rows * span + 1, width, 2 * width), jnp.bfloat16)
    near = [pltpu.with_memory_space_constraint(x, pltpu.VMEM) for x in before]
    return pl.pallas_call(
        functools.partial(table_kernel, rows, width, span, jobs, count, not before),
        out_shape=(kind, kind),
        in_specs=[pl.BlockSpec(memory_space=pltpu.SMEM)]
        + [pl.BlockSpec(memory_space=pl.ANY)] * count
        + [pl.BlockSpec(memory_space=pltpu.VMEM)] * len(before),
        out_specs=(pl.BlockSpec(memory_space=pltpu.VMEM),) * 2,
        scratch_shapes=[
            pltpu.VMEM((len(jobs), rows, width, wide), jnp.float32),
            pltpu.SemaphoreType.DMA((len(jobs), 2)),
        ],
        input_output_aliases={1 + count + i: i for i in range(len(before))},
        compiler_params=pltpu.CompilerParams(vmem_limit_bytes=TABLE_BYTES),
        cost_estimate=pl.CostEstimate(flops=2 * 10**9, bytes_accessed=10**7, transcendentals=0),
    )(flags, *panels, *near)


def product_kernel(first, begin, end, width, span, pick_ref, flag_ref, high, low, *refs):
    left = refs[:5]
    out_ref, left_buf, left_sem = refs[5:]

    def bring(place, src):
        rows_here = src.at[pl.ds(begin, end - begin)]
        return pltpu.make_async_copy(rows_here, left_buf.at[place - first], left_sem.at[place - first])

    for place in range(first, 3):
        bring(place, left[place]).start()

    @pl.when(flag_ref[0] == 1)
    def _():
        bring(3, left[3]).start()

    @pl.when(flag_ref[0] == 0)
    def _():
        bring(3, left[4]).start()

    for place in range(first, 4):
        bring(place, left[3]).wait()

    lane = lax.broadcasted_iota(jnp.int32, (width, 2 * width), 1) < width

    def one_row(row):
        both = jnp.zeros((2 * width, span * width), jnp.float32)
        single = jnp.zeros((width, span * width), jnp.float32)
        for place in range(4):
            top_rows, low_rows = [], []
            for k in range(span):
                at = ((row * 4 + place) * span + k) * span
                picks = [pick_ref[at + m] for m in range(span)]
                for entries, rows_of in ((high, top_rows), (low, low_rows)):
                    rows_of.append(
                        jnp.concatenate(
                            [
                                jnp.where(lane, entries[picks[0]], entries[picks[1]]),
                                jnp.where(lane, entries[picks[2]], entries[picks[3]]),
                            ],
                            axis=1,
                        )
                    )
            x = left[place][row] if place < first else left_buf[place - first, row - begin]
            top = x.astype(jnp.bfloat16)
            rest = (x - top.astype(jnp.float32)).astype(jnp.bfloat16)
            both += jnp.dot(
                jnp.concatenate([top, rest], axis=0),
                jnp.concatenate(top_rows, axis=0),
                preferred_element_type=jnp.float32,
            )
            single += jnp.dot(
                top, jnp.concatenate(low_rows, axis=0), preferred_element_type=jnp.float32
            )
        out_ref[row - begin] = both[:width] + both[width:] + single

    @pl.loop(0, (end - begin) // ROW_STEP)
    def _(step):
        for j in range(ROW_STEP):
            one_row(begin + step * ROW_STEP + j)


def product(left, tables, picks, flags, begin, end, first=0):
    rows, width, wide = left[0].shape
    span = wide // width
    near = [pltpu.with_memory_space_constraint(x, pltpu.VMEM) for x in (*tables, *left[:first])]
    return pl.pallas_call(
        functools.partial(product_kernel, first, begin, end, width, span),
        out_shape=jax.ShapeDtypeStruct((end - begin, width, wide), jnp.float32),
        in_specs=[pl.BlockSpec(memory_space=pltpu.SMEM)] * 2
        + [pl.BlockSpec(memory_space=pltpu.VMEM)] * len(near)
        + [pl.BlockSpec(memory_space=pl.ANY)] * (5 - first),
        out_specs=pl.BlockSpec(memory_space=pltpu.VMEM),
        scratch_shapes=[
            pltpu.VMEM((4 - first, end - begin, width, wide), jnp.float32),
            pltpu.SemaphoreType.DMA((4 - first,)),
        ],
        compiler_params=pltpu.CompilerParams(vmem_limit_bytes=PRODUCT_BYTES),
        cost_estimate=pl.CostEstimate(flops=8 * 10**9, bytes_accessed=10**7, transcendentals=0),
    )(picks, flags, *near, *left[first:])


def spread_kernel(layers, groups, cap, wide, src, dst):
    for group in range(groups):
        for slot in range(cap):
            block = src[slot, :, group * wide : (group + 1) * wide]
            for layer in range(layers):
                dst[(layer * groups + group) * cap + slot] = block


def spread(owner_blocks, layers, groups):
    cap, width, total = owner_blocks.shape
    wide = total // groups
    return pl.pallas_call(
        functools.partial(spread_kernel, layers, groups, cap, wide),
        out_shape=jax.ShapeDtypeStruct((layers * groups * cap, width, wide), jnp.float32),
        in_specs=[pl.BlockSpec(memory_space=pltpu.VMEM)],
        out_specs=pl.BlockSpec(memory_space=pltpu.VMEM),
        compiler_params=pltpu.CompilerParams(vmem_limit_bytes=SPREAD_BYTES),
    )(owner_blocks)


def pick_table(block_cols, out_cols, grid_row, grid_col, core, y, z, rows, span):
    cols = block_cols.reshape(N_GROUP, rows, N_GROUP, span)
    left_cols = lax.dynamic_slice(block_cols, (grid_row * rows, 0), (rows, N_GROUP * span))
    left_cols = left_cols.reshape(rows, N_GROUP, span)
    z_from = (z + jnp.array([0, 3, 1, 2], dtype=jnp.int32)) % N_Z
    groups = (core + z_from) % 2 * N_Z + z_from
    names = jnp.arange(N_GROUP, dtype=jnp.int32)
    chosen = (groups[:, None] == names[None, :]).astype(jnp.int32)
    local = left_cols - names[None, :, None] * rows
    slots = jnp.sum(local[:, None] * chosen[None, :, :, None], axis=2)
    right_cols = jnp.sum(
        cols * (names == grid_col).astype(jnp.int32)[None, None, :, None], axis=2
    )
    right_cols = jnp.sum(right_cols[None] * chosen[:, :, None, None], axis=1)
    hit = (slots[..., None] == jnp.arange(rows, dtype=jnp.int32)).astype(jnp.int32)
    found = jnp.sum(hit[..., None] * right_cols[None, :, None], axis=3)
    place = (groups // 2 - y) % N_Y
    base = ((place[None, :, None] * rows + slots) * 2)[..., None]
    match = found[..., :, None] == out_cols[:, None, None, None, :]
    piece = jnp.arange(span, dtype=jnp.int32)
    swap = (piece[:, None] + piece[None, :]) % 2
    entry = (base[..., None] + (piece // 2)[:, None]) * 2 + swap
    none = 4 * rows * span
    picked = none + jnp.sum(jnp.where(match, entry - none, 0), axis=3)
    return picked.reshape(-1).astype(jnp.int32)


def body(owner_blocks, owner_counts, block_cols, filter_mask, gamma):
    layer = lax.axis_index("layer")
    grid_row = lax.axis_index("row")
    grid_col = lax.axis_index("col")
    y, core = grid_row // N_CORE, grid_row % N_CORE
    q, z = grid_col // N_Z, grid_col % N_Z
    part = (layer + q) % 2
    cap, width, _ = owner_blocks.shape
    span = N_SLOT
    rows = block_cols.shape[0] // N_GROUP

    counts = owner_counts[0]
    ends = jnp.cumsum(counts)
    local = jnp.arange(rows, dtype=jnp.int32)
    which = jnp.sum((ends[None, :] <= local[:, None]).astype(jnp.int32), axis=1)
    slot = local - (jnp.take(ends, which) - jnp.take(counts, which))
    source = which * cap + slot
    plain_send = spread(owner_blocks, N_LAYER, N_GROUP)
    plain_got = lax.all_to_all(
        plain_send, ("layer", "col"), split_axis=0, concat_axis=0, tiled=True
    )
    row_here = 2 * y + part
    out_cols = lax.dynamic_slice(block_cols, (row_here * rows, grid_col * span), (rows, span))
    keep = lax.dynamic_slice(filter_mask, (row_here * rows, grid_col * span), (rows, span))
    picks = pick_table(block_cols, out_cols, row_here, grid_col, core, y, z, rows, span)
    flags = jnp.stack([core == (z + q) % 2, core != (part + y // 2) % 2, y >= 2]).astype(jnp.int32)

    keep_wide = jnp.repeat(keep.astype(jnp.float32), width, axis=1)[:, None, :]
    own = (out_cols == (row_here * rows + local)[:, None]).astype(jnp.float32)
    plain_got, source, picks, flags, keep_wide, own = lax.optimization_barrier(
        (plain_got, source, picks, flags, keep_wide, own)
    )
    density = plain_got.at[source].get(mode="promise_in_bounds")

    left, right = gather_first(density)
    mine = jnp.where(core == part, density, right[5])
    density, above, first, below, second, swapped = right
    jobs = ((0, (0, 1), 2), (1, (2,), None), (3, (3,), None))
    tables = table((swapped, density, above, below), jobs, flags, rows)
    tables = table((first, second), ((2, (0, 1), None),), flags, rows, tables)
    partial_value = product(left, tables, picks, flags, 0, rows, 3)
    square = partial_value + swap_cores(partial_value)
    square = square * keep_wide
    unit = (own[:, None, :, None] * jnp.eye(width, dtype=jnp.float32)[None, :, None, :]).reshape(
        rows, width, span * width
    )
    mix = gamma[0]
    mixed = mix * unit + (4.0 - 2.0 * mix) * mine + (mix - 3.0) * square

    left, right = gather_second(square, mixed)
    own_right, above, across, below, pair = right
    jobs = ((0, (0,), None), (2, (1, 2), 1))
    tables = table((own_right, across, pair), jobs, flags, rows)
    tables = table((above, below), ((1, (0,), None), (3, (1,), None)), flags, rows, tables)

    def output(layer, y, core, q, z):
        return (1 - layer, y, core, q, z) if core == layer ^ q else None

    half = rows // 2
    totals = [product(left, tables, picks, flags, begin, begin + half, 3) for begin in (0, half)]
    totals = [total + swap_cores(total) for total in totals]
    outs = [jnp.where(core == part, total, send(total, output)) for total in totals]
    return jnp.concatenate(outs, axis=0)


def solution(mesh):
    placed = (P(("layer", "row", "col"), None, None), P("row", None), P(), P(), P())
    return jax.shard_map(
        body, mesh=mesh, in_specs=placed, out_specs=P("row", None, "col"), check_vma=False
    )
```
